32 devices in a mesh: dom: 8 (over z, core), blk: 4 (over y, x).
Axes of the slice: x: 2, y: 2, z: 4, core: 2. Of those that a mesh axis runs over, the one named last changes fastest.
Arguments:
- images: bfloat16 [512, 128, 256], P('dom', 'blk'), may hold values from -4.5 to 6.5
- ref_store: bfloat16 [8, 16, 4, 128, 256], P('dom', None, None, 'blk'), may hold values from -0.03125 to 0.03125
- block_owner: int32 [16], replicated, may hold values from 0 to 7, as said below
- class_gain: float32 [64], replicated, may hold values from 0.5 to 2
- precision: float32 [512], P('dom'), may hold values from 0.5 to 80
Outputs:
- class_sums: float32 [8, 2, 4, 128, 256], P('dom', None, None, 'blk')
The draws below stay inside these ranges and needn't reach their ends.
Inputs may be any that keep to these rules, and one draw needn't show every extreme that they name: `block_owner`: each index d of dom owns exactly 2 blocks.
All inputs are finite; a program needn't handle non-finite values.
Results may differ from the reference program's by a relative error of at most 0.0049.
Values may be sent and summed in bfloat16 or wider, within the bound.
A program may use at most 64 MiB of HBM per device.

```python
import math
import jax
import jax.numpy as jnp

R = 128
A = 256
S = 64
K = 64
NBLK = 16
KB = 4
BLK_PER = 2
PARTICLES = 512
ROT_STEP = 4
N_DOM = 8


def draw_block_owner(key, part):
    shuffled = jax.random.permutation(key, NBLK)
    return (shuffled // BLK_PER).astype(jnp.int32)


def draw_images(key, part):
    cycle_key = jax.random.fold_in(key, 11)
    noise_key = jax.random.fold_in(key, 12)
    cycle_level = jax.random.uniform(cycle_key, (1, R, 1), jnp.float32, 0.5, 1.5)
    noise = jax.random.truncated_normal(noise_key, -5.0, 5.0, (PARTICLES, R, A), jnp.float32)
    return (noise + cycle_level).astype(jnp.bfloat16)


def draw_precision(key, part):
    base_key = jax.random.fold_in(key, 21)
    fraction = jax.random.uniform(base_key, (PARTICLES,), jnp.float32)
    values = jnp.exp(math.log(0.8) + fraction * (math.log(1.6) - math.log(0.8)))
    return values.astype(jnp.float32)


def block_levels(key, shape, shards, smallest, top_value):
    loudness = 1.0
    for dim, shards_of in shards:
        draws = jax.random.uniform(jax.random.fold_in(jax.random.fold_in(key, 6), dim), (shards_of,), jnp.float32, smallest / len(shards), top_value / len(shards))
        loudness = loudness * jnp.repeat(jnp.exp(draws), shape[dim] // shards_of).reshape((-1,) + (1,) * (len(shape) - 1 - dim))
    return loudness


def normal_values(rng, extent, scale, reach, cuts=(), kind=jnp.bfloat16):
    level = block_levels(rng, extent, cuts, -0.22, 0.18) if cuts else 1.0
    array = jax.random.normal(rng, extent, jnp.float32) * scale * level
    return jnp.minimum(jnp.maximum(array, -reach), reach).astype(kind)


def setup_inputs(seed: int = 0) -> dict:
    streams_of = jax.random.split(jax.random.key(seed), 6)
    images = draw_images(jax.random.fold_in(streams_of[5], 71), 0)
    ref_store = normal_values(streams_of[1], (N_DOM, NBLK, KB, R, A), (R * A) ** -0.5, 0.03125, ((0, 8), (3, 4)))
    block_owner = draw_block_owner(jax.random.fold_in(streams_of[5], 71), 0)
    class_gain = jnp.clip(jnp.exp(jax.random.uniform(streams_of[3], (K,), jnp.float32, math.log(0.5), math.log(2.0))), 0.5, 2.0)
    precision = draw_precision(jax.random.fold_in(streams_of[5], 71), 0)
    return dict(images=images, ref_store=ref_store, block_owner=block_owner, class_gain=class_gain, precision=precision)


def reference(images, ref_store, block_owner, class_gain, precision):
    block_ids = jnp.arange(NBLK, dtype=jnp.int32)
    stored = ref_store[block_owner, block_ids]
    references = (stored.astype(jnp.float32) * class_gain.reshape(NBLK, KB, 1, 1)).astype(jnp.bfloat16)
    ref_float = references.astype(jnp.float32).reshape(K, R, A)
    norm_sums = jnp.sum(ref_float * ref_float, axis=(1, 2))
    image_float = images.astype(jnp.float32)
    image_spec = jnp.fft.rfft(image_float, axis=-1)
    ref_spec = jnp.fft.rfft(ref_float, axis=-1)
    cross_spec = jnp.einsum('prf,krf->pkf', jnp.conj(image_spec), ref_spec)
    correlation = jnp.fft.irfft(cross_spec, n=A, axis=-1)[:, :, ::ROT_STEP]
    logits = precision[:, None, None] * (correlation - 0.5 * norm_sums[None, :, None])
    flat_logits = logits.reshape(PARTICLES, K * S)
    row_max = jnp.max(flat_logits, axis=1, keepdims=True)
    exponent = jnp.exp(flat_logits - row_max)
    weights = exponent / jnp.sum(exponent, axis=1, keepdims=True)
    weight_float = weights.reshape(PARTICLES, K, S)
    weight_full = jnp.zeros((PARTICLES, K, A), jnp.float32).at[:, :, ::ROT_STEP].set(weight_float)
    weight_spec = jnp.fft.rfft(weight_full, axis=-1)
    total_spec = jnp.einsum('pkf,prf->krf', weight_spec, image_spec)
    totals = jnp.fft.irfft(total_spec, n=A, axis=-1).astype(jnp.float32)
    owner_order = jnp.argsort(block_owner, stable=True).astype(jnp.int32)
    blocked = totals.reshape(NBLK, KB, R, A)[owner_order]
    return blocked.reshape(N_DOM, BLK_PER, KB, R, A)
```

```python
import functools
import jax
import jax.numpy as jnp
from jax import lax
from jax.experimental import pallas as pl
from jax.experimental.pallas import tpu as pltpu
from jax.sharding import PartitionSpec as P

S = 64
S1 = 8
S2 = 8
G = 4
NT = (((1,), (1,)), ((), ()))


def roll_cycles(x, shift, angles):
    shift = shift % angles
    if shift == 0:
        return x
    parts = [
        pltpu.roll(x[:, c * angles : (c + 1) * angles], shift, 1)
        for c in range(x.shape[1] // angles)
    ]
    return jnp.concatenate(parts, axis=1)


def correlate_kernel(angles, step, img_ref, ref_ref, rolled_ref, score_ref, flat, turned):
    n_dom, _, own, _ = ref_ref.shape
    rows = img_ref.shape[1]
    classes = n_dom * own
    x = img_ref[0].astype(jnp.float32)
    for s1 in range(S1):
        rolled_ref[0, s1 * rows : (s1 + 1) * rows, :] = roll_cycles(
            x, step * s1, angles
        ).astype(jnp.bfloat16)
    for d in range(n_dom):
        flat[d * own : (d + 1) * own, :] = ref_ref[d, 0].astype(jnp.float32)
    y = flat[...]
    half_norm = 0.5 * jnp.sum(y * y, axis=1, keepdims=True)
    for s2 in range(S2):
        turned[s2 * classes : (s2 + 1) * classes, :] = roll_cycles(
            y, -step * S1 * s2, angles
        ).astype(jnp.bfloat16)

    @pl.when(pl.program_id(0) == 0)
    def _():
        score_ref[...] = jnp.zeros_like(score_ref)

    products = lax.dot_general(
        turned[...], rolled_ref[0], NT, preferred_element_type=jnp.float32
    )
    score_ref[...] += products - jnp.tile(half_norm, (S2, 1))


def totals_kernel(angles, step, own, prec_ref, score_ref, rolled_ref, out_ref, high, low):
    rows = score_ref.shape[0]
    classes = rows // S2

    @pl.when(pl.program_id(0) == 0)
    def _():
        logits = score_ref[...] * prec_ref[...]
        top = jnp.max(logits, axis=0, keepdims=True)
        span = top.shape[1] // S1
        top = functools.reduce(
            jnp.maximum, [top[:, i * span : (i + 1) * span] for i in range(S1)]
        )
        e = jnp.exp(logits - jnp.tile(top, (1, S1)))
        mass = jnp.sum(e, axis=0, keepdims=True)
        mass = functools.reduce(
            jnp.add, [mass[:, i * span : (i + 1) * span] for i in range(S1)]
        )
        w = e * jnp.tile(1.0 / mass, (1, S1))
        hi = w.astype(jnp.bfloat16)
        high[...] = hi
        low[...] = (w - hi.astype(jnp.float32)).astype(jnp.bfloat16)

    x = rolled_ref[0]
    spread = jnp.dot(high[...], x, preferred_element_type=jnp.float32)
    spread += jnp.dot(low[...], x, preferred_element_type=jnp.float32)
    running = spread[(S2 - 1) * classes :, :]
    for s2 in reversed(range(S2 - 1)):
        running = (
            roll_cycles(running, step * S1, angles)
            + spread[s2 * classes : (s2 + 1) * classes, :]
        )
    for d in range(classes // own):
        out_ref[d, 0] = running[d * own : (d + 1) * own, :]


def shards(images, ref_store, block_owner, class_gain, precision):
    particles, cycles, angles = images.shape
    n_dom = lax.axis_size("dom")
    blocks = block_owner.shape[0]
    per_block = ref_store.shape[2]
    owned = blocks // n_dom
    own = owned * per_block
    classes = blocks * per_block
    step = angles // S
    groups = cycles // G
    wide = G * angles
    stored = ref_store[0]

    match = block_owner == lax.axis_index("dom")
    ids = jnp.arange(blocks, dtype=jnp.int32)
    rank = jnp.sum(match[None, :] & (ids[None, :] < ids[:, None]), axis=1)
    gains = class_gain.reshape(blocks, per_block)
    picked = []
    for j in range(owned):
        b = jnp.sum(jnp.where(match & (rank == j), ids, 0))
        block = lax.dynamic_index_in_dim(stored, b, 0, keepdims=False)
        gain = lax.dynamic_index_in_dim(gains, b, 0, keepdims=False)
        picked.append(block.astype(jnp.float32) * gain[:, None, None])
    mine = jnp.concatenate(picked, 0).astype(jnp.bfloat16)
    mine = mine.reshape(own, groups, wide).transpose(1, 0, 2)
    refs = lax.all_gather(mine, "dom", axis=0, tiled=False)
    grouped = images.reshape(particles, groups, wide).transpose(1, 0, 2)

    lhs = S2 * classes
    rhs = S1 * particles
    rolled, scores = pl.pallas_call(
        functools.partial(correlate_kernel, angles, step),
        grid=(groups,),
        in_specs=[
            pl.BlockSpec((1, particles, wide), lambda g: (g, 0, 0)),
            pl.BlockSpec((n_dom, 1, own, wide), lambda g: (0, g, 0, 0)),
        ],
        out_specs=[
            pl.BlockSpec((1, rhs, wide), lambda g: (g, 0, 0)),
            pl.BlockSpec((lhs, rhs), lambda g: (0, 0)),
        ],
        out_shape=[
            jax.ShapeDtypeStruct((groups, rhs, wide), jnp.bfloat16),
            jax.ShapeDtypeStruct((lhs, rhs), jnp.float32),
        ],
        scratch_shapes=[
            pltpu.VMEM((classes, wide), jnp.float32),
            pltpu.VMEM((lhs, wide), jnp.bfloat16),
        ],
        compiler_params=pltpu.CompilerParams(vmem_limit_bytes=48 * 1024 * 1024),
        name="correlate",
    )(grouped, refs)
    scores = lax.psum(scores, "blk")
    prec = jnp.tile(precision, S1)[None, :]
    parts = pl.pallas_call(
        functools.partial(totals_kernel, angles, step, own),
        grid=(groups,),
        in_specs=[
            pl.BlockSpec((1, rhs), lambda g: (0, 0)),
            pl.BlockSpec((lhs, rhs), lambda g: (0, 0)),
            pl.BlockSpec((1, rhs, wide), lambda g: (g, 0, 0)),
        ],
        out_specs=pl.BlockSpec((n_dom, 1, own, wide), lambda g: (0, g, 0, 0)),
        out_shape=jax.ShapeDtypeStruct((n_dom, groups, own, wide), jnp.float32),
        scratch_shapes=[
            pltpu.VMEM((lhs, rhs), jnp.bfloat16),
            pltpu.VMEM((lhs, rhs), jnp.bfloat16),
        ],
        compiler_params=pltpu.CompilerParams(vmem_limit_bytes=48 * 1024 * 1024),
        name="totals",
    )(prec, scores, rolled)
    mine_sum = lax.psum_scatter(parts, "dom", scatter_dimension=0, tiled=True)[0]
    mine_sum = mine_sum.transpose(1, 0, 2).reshape(owned, per_block, cycles, angles)
    return mine_sum[None]


def solution(mesh):
    return jax.shard_map(
        shards,
        mesh=mesh,
        in_specs=(P("dom", "blk", None), P("dom", None, None, "blk", None), P(), P(), P("dom")),
        out_specs=P("dom", None, None, "blk", None),
        check_vma=False,
    )
```

```python
import functools
import jax
import jax.numpy as jnp
from jax import lax
from jax.experimental import pallas as pl
from jax.experimental.pallas import tpu as pltpu
from jax.sharding import PartitionSpec as P

S = 64
S1 = 8
S2 = 8
G = 4
UNIT = 16
PIECES = 4
NT = (((1,), (1,)), ((), ()))
MESH = pl.DeviceIdType.MESH


def roll_cycles(x, shift, angles):
    shift = shift % angles
    if shift == 0:
        return x
    parts = [
        pltpu.roll(x[:, c * angles : (c + 1) * angles], shift, 1)
        for c in range(x.shape[1] // angles)
    ]
    return jnp.concatenate(parts, axis=1)


def spread_lanes(op, x, width):
    shift = width
    while shift < x.shape[1]:
        x = op(x, pltpu.roll(x, shift, 1))
        shift *= 2
    return x


def kernel(
    n_dom, n_blk, angles, per_block, owned,
    owner_ref, gain_ref, prec_ref, img_ref, store_ref, out_ref,
    minef, refs, rolled, turned, flat, norm, scores, got, weights, parts, sib, zout, zin,
    ref_send, ref_recv, fwd_send, score_send, score_recv, w_send, w_recv,
    sib_send, sib_recv, z_send, z_recv,
):
    step = angles // S
    own = owned * per_block
    chips = n_dom // 2
    unit_devs = UNIT // own
    units = n_dom // unit_devs
    groups, particles, wide = img_ref.shape
    pp = particles // n_blk
    blocks = store_ref.shape[0]
    me = lax.axis_index("dom")
    blk = lax.axis_index("blk")
    chip = me // 2
    core = me % 2
    sibling = chip * 2 + 1 - core
    far = [lax.rem(chip + o, chips) for o in range(1, chips)]
    pair = blk // 2
    blk_peers = [(1 - pair) * 2, (1 - pair) * 2 + 1, pair * 2 + 1 - blk % 2]

    barrier = pltpu.get_barrier_semaphore()
    for c in far:
        pl.semaphore_signal(barrier, inc=1, device_id={"dom": c * 2 + core}, device_id_type=MESH)
    pl.semaphore_signal(barrier, inc=1, device_id={"dom": sibling}, device_id_type=MESH)
    for b in blk_peers:
        pl.semaphore_signal(barrier, inc=1, device_id={"blk": b}, device_id_type=MESH)

    picks = [jnp.int32(0)] * owned
    seen = jnp.int32(0)
    for b in range(blocks):
        hit = (owner_ref[b] == me).astype(jnp.int32)
        for j in range(owned):
            take = jnp.logical_and(hit == 1, seen == j)
            picks[j] = jnp.where(take, jnp.int32(b), picks[j])
        seen = seen + hit
    for j in range(owned):
        block = store_ref[picks[j]].astype(jnp.float32)
        row = lax.broadcasted_iota(jnp.int32, block.shape, 0) & (per_block - 1)
        gain = jnp.zeros_like(block)
        for i in range(per_block):
            gain = jnp.where(row == i, gain_ref[picks[j] * per_block + i], gain)
        block = block * gain
        for g in range(groups):
            at = (g % 2) * own + j * per_block
            minef[g // 2, at : at + per_block, :] = block[g * per_block : (g + 1) * per_block, :]
    refs[me] = minef[...].astype(jnp.bfloat16)

    pl.semaphore_wait(barrier, len(far) + 1 + len(blk_peers))

    def ref_copy(slot, target, send):
        return pltpu.make_async_remote_copy(
            src_ref=refs.at[slot], dst_ref=refs.at[slot], send_sem=send,
            recv_sem=ref_recv.at[slot], device_id={"dom": target}, device_id_type=MESH,
        )

    out_copies = [ref_copy(me, c * 2 + core, ref_send.at[o]) for o, c in enumerate(far)]
    out_copies.append(ref_copy(me, sibling, ref_send.at[chips - 1]))
    for copy in out_copies:
        copy.start()

    def roll_images(g, carry):
        x = img_ref[g].astype(jnp.float32)
        for s1 in range(S1):
            r = roll_cycles(x, step * s1, angles).astype(jnp.bfloat16)
            for j in range(n_blk):
                at = j * pp * S1 + s1 * pp
                rolled[g, at : at + pp, :] = r[j * pp : (j + 1) * pp, :]
        return carry

    lax.fori_loop(0, groups, roll_images, 0)
    norm[...] = jnp.zeros_like(norm)

    fwd = []
    for o, c in enumerate(far):
        slot = c * 2 + core
        ref_copy(slot, slot, ref_send.at[o]).wait_recv()
        copy = ref_copy(slot, sibling, fwd_send.at[o])
        copy.start()
        fwd.append(copy)
    ref_copy(sibling, sibling, ref_send.at[chips - 1]).wait_recv()
    for o, c in enumerate(far):
        slot = c * 2 + 1 - core
        ref_copy(slot, sibling, fwd_send.at[o]).wait_recv()

    def turn_refs(gp, carry):
        for u in range(units):
            for e in range(unit_devs):
                y = refs[u * unit_devs + e, gp].astype(jnp.float32)
                for h in range(2):
                    flat[u, h, e * own : (e + 1) * own, :] = y[h * own : (h + 1) * own, :]
            for h in range(2):
                y = flat[u, h]
                half = 0.5 * jnp.sum(y * y, axis=1, keepdims=True)
                norm[u] += jnp.broadcast_to(half, (UNIT, norm.shape[2]))
                for s2 in range(S2):
                    at = u * S2 * UNIT + s2 * UNIT
                    turned[gp * 2 + h, at : at + UNIT, :] = roll_cycles(
                        y, -step * S1 * s2, angles
                    ).astype(jnp.bfloat16)
        return carry

    lax.fori_loop(0, groups // 2, turn_refs, 0)

    lanes = pp * S1

    def score_pair(which):
        first = which * 2
        for i in range(2):
            for u in range(units):
                for s2 in range(S2):
                    at = u * S2 * UNIT + s2 * UNIT
                    scores[first + i, at : at + UNIT, :] = -norm[u]

        def body(g, carry):
            cols = rolled[g, pl.ds(pl.multiple_of(which * 2 * lanes, 2 * lanes), 2 * lanes), :]
            prod = lax.dot_general(turned[g], cols, NT, preferred_element_type=jnp.float32)
            for i in range(2):
                scores[first + i] += prod[:, i * lanes : (i + 1) * lanes]
            return carry

        lax.fori_loop(0, groups, body, 0)

    def score_copy(src, slot, target, o):
        return pltpu.make_async_remote_copy(
            src_ref=scores.at[src], dst_ref=got.at[slot], send_sem=score_send.at[o],
            recv_sem=score_recv.at[slot], device_id={"blk": target}, device_id_type=MESH,
        )

    score_copies = [score_copy(b, blk, b, o) for o, b in enumerate(blk_peers)]
    score_pair(1 - pair)
    score_copies[1].start()
    score_copies[0].start()
    score_pair(pair)
    score_copies[2].start()
    for o in (2, 0, 1):
        b = blk_peers[o]
        score_copy(b, b, b, o).wait_recv()
    total = scores[blk]
    for b in blk_peers:
        total = total + got[b]
    logits = total * prec_ref[blk][0:1, :]
    top = jnp.broadcast_to(jnp.max(logits, axis=0, keepdims=True), (8, lanes))
    top = spread_lanes(jnp.maximum, top, pp)[0:1, :]
    e = jnp.exp(logits - top)
    mass = jnp.broadcast_to(jnp.sum(e, axis=0, keepdims=True), (8, lanes))
    mass = spread_lanes(jnp.add, mass, pp)[0:1, :]
    weights[blk] = (e * (1.0 / mass)).astype(jnp.bfloat16)

    def w_copy(slot, target, o):
        return pltpu.make_async_remote_copy(
            src_ref=weights.at[slot], dst_ref=weights.at[slot], send_sem=w_send.at[o],
            recv_sem=w_recv.at[slot], device_id={"blk": target}, device_id_type=MESH,
        )

    w_copies = [w_copy(blk, b, o) for o, b in enumerate(blk_peers)]
    for o in (1, 0, 2):
        w_copies[o].start()
    for o, b in enumerate(blk_peers):
        w_copy(b, b, o).wait_recv()

    per_piece = groups // PIECES

    def sib_copy(q, which):
        return pltpu.make_async_remote_copy(
            src_ref=parts.at[which, q], dst_ref=sib.at[q], send_sem=sib_send.at[q],
            recv_sem=sib_recv.at[q], device_id={"dom": sibling}, device_id_type=MESH,
        )

    def z_copy(q, src, slot, target, o):
        return pltpu.make_async_remote_copy(
            src_ref=zout.at[q, src], dst_ref=zin.at[q, slot], send_sem=z_send.at[q, o],
            recv_sem=z_recv.at[q, slot], device_id={"dom": target * 2 + core}, device_id_type=MESH,
        )

    sib_copies, z_copies = [], []
    for q in range(PIECES + 1):
        if q < PIECES:

            def body(gi, carry, q=q):
                w = jnp.concatenate([weights[j] for j in range(n_blk)], axis=1)
                spread = jnp.dot(
                    w, rolled[q * per_piece + gi], preferred_element_type=jnp.float32
                )
                for u in range(units):
                    base = u * S2 * UNIT
                    running = spread[base + (S2 - 1) * UNIT : base + S2 * UNIT, :]
                    for s2 in reversed(range(S2 - 1)):
                        running = (
                            roll_cycles(running, step * S1, angles)
                            + spread[base + s2 * UNIT : base + (s2 + 1) * UNIT, :]
                        )
                    for k in range(unit_devs):
                        d = u * unit_devs + k
                        parts[d % 2, q, d // 2, gi] = running[k * own : (k + 1) * own, :]
                return carry

            lax.fori_loop(0, per_piece, body, 0)
            copy = sib_copy(q, 1 - core)
            copy.start()
            sib_copies.append(copy)
        if q >= 1:
            p = q - 1
            sib_copy(p, 1 - core).wait_recv()
            for c in range(chips):
                both = parts[core, p, c] + sib[p, c]
                parts[core, p, c] = both
                zout[p, c] = both.reshape(per_piece * own, wide).astype(jnp.bfloat16)
            for o, c in enumerate(far):
                copy = z_copy(p, c, chip, c, o)
                copy.start()
                z_copies.append(copy)

    for q in range(PIECES):
        total = parts[core, q, chip].reshape(per_piece * own, wide)
        for o, c in enumerate(far):
            z_copy(q, c, c, c, o).wait_recv()
            total = total + zin[q, c].astype(jnp.float32)
        for gi in range(per_piece):
            for rr in range(G):
                out_ref[:, (q * per_piece + gi) * G + rr, :] = total[
                    gi * own : (gi + 1) * own, rr * angles : (rr + 1) * angles
                ]

    for copy in out_copies + fwd + score_copies + w_copies + sib_copies + z_copies:
        copy.wait_send()


def shards(images, ref_store, block_owner, class_gain, precision):
    particles, cycles, angles = images.shape
    n_dom = lax.axis_size("dom")
    n_blk = lax.axis_size("blk")
    blocks = block_owner.shape[0]
    per_block = ref_store.shape[2]
    owned = blocks // n_dom
    own = owned * per_block
    classes = blocks * per_block
    groups = cycles // G
    wide = G * angles
    chips = n_dom // 2
    units = classes // UNIT
    pp = particles // n_blk
    lhs = S2 * classes
    rhs = S1 * particles
    per_piece = groups // PIECES

    grouped = images.reshape(particles, groups, wide).transpose(1, 0, 2)
    store = ref_store[0].reshape(blocks, per_block, groups, wide).transpose(0, 2, 1, 3)
    store = store.reshape(blocks, groups * per_block, wide)
    prec = jnp.tile(precision.reshape(n_blk, 1, pp), (1, 8, S1))

    vmem = pl.BlockSpec(memory_space=pltpu.VMEM)
    smem = pl.BlockSpec(memory_space=pltpu.SMEM)
    bf16, f32 = jnp.bfloat16, jnp.float32
    dma = pltpu.SemaphoreType.DMA
    out = pl.pallas_call(
        functools.partial(kernel, n_dom, n_blk, angles, per_block, owned),
        in_specs=[smem, smem, vmem, vmem, vmem],
        out_specs=vmem,
        out_shape=jax.ShapeDtypeStruct((own, cycles, angles), f32),
        scratch_shapes=[
            pltpu.VMEM((groups // 2, 2 * own, wide), f32),
            pltpu.VMEM((n_dom, groups // 2, 2 * own, wide), bf16),
            pltpu.VMEM((groups, rhs, wide), bf16),
            pltpu.VMEM((groups, lhs, wide), bf16),
            pltpu.VMEM((units, 2, UNIT, wide), f32),
            pltpu.VMEM((units, UNIT, pp * S1), f32),
            pltpu.VMEM((n_blk, lhs, pp * S1), f32),
            pltpu.VMEM((n_blk, lhs, pp * S1), f32),
            pltpu.VMEM((n_blk, lhs, pp * S1), bf16),
            pltpu.VMEM((2, PIECES, chips, per_piece, own, wide), f32),
            pltpu.VMEM((PIECES, chips, per_piece, own, wide), f32),
            pltpu.VMEM((PIECES, chips, per_piece * own, wide), bf16),
            pltpu.VMEM((PIECES, chips, per_piece * own, wide), bf16),
            dma((chips,)), dma((n_dom,)), dma((chips,)),
            dma((n_blk,)), dma((n_blk,)), dma((n_blk,)), dma((n_blk,)),
            dma((PIECES,)), dma((PIECES,)), dma((PIECES, chips)), dma((PIECES, chips)),
        ],
        compiler_params=pltpu.CompilerParams(
            collective_id=0, has_side_effects=True, vmem_limit_bytes=52 * 1024 * 1024
        ),
        cost_estimate=pl.CostEstimate(
            flops=4 * lhs * rhs * groups * wide, bytes_accessed=4 * 1024 * 1024, transcendentals=0
        ),
        name="fused",
    )(block_owner, class_gain, prec, grouped, store)
    return out.reshape(1, owned, per_block, cycles, angles)


def solution(mesh):
    return jax.shard_map(
        shards,
        mesh=mesh,
        in_specs=(P("dom", "blk", None), P("dom", None, None, "blk", None), P(), P(), P("dom")),
        out_specs=P("dom", None, None, "blk", None),
        check_vma=False,
    )
```

```python
import functools
import jax
import jax.numpy as jnp
from jax import lax
from jax.experimental import pallas as pl
from jax.experimental.pallas import tpu as pltpu
from jax.sharding import PartitionSpec as P

S = 64
S1 = 8
S2 = 8
G = 4
PIECES = 4
LANES = 128
NT = (((1,), (1,)), ((), ()))
MESH = pl.DeviceIdType.MESH


def roll_cycles(x, shift, angles):
    shift = shift % angles
    if shift == 0:
        return x
    parts = [
        pltpu.roll(x[:, c * angles : (c + 1) * angles], shift, 1)
        for c in range(x.shape[1] // angles)
    ]
    return jnp.concatenate(parts, axis=1)


def every(ref, start, count, stride):
    return jnp.concatenate(
        [ref[h, pl.ds(start, count, stride=stride), :] for h in range(ref.shape[0])], axis=1
    )


def spread_lanes(op, x, width):
    shift = width
    while shift < x.shape[1]:
        x = op(x, pltpu.roll(x, shift, 1))
        shift *= 2
    return x


def kernel(
    n_dom, n_blk, angles, per_block, owned,
    owner_ref, gain_ref, prec_ref, img_ref, store_ref, out_ref,
    imgf, blockf, minef, refs, rolled, turned, flat, norm, scores, got, weights, parts, sib, zout, zin,
    ref_send, ref_recv, fwd_send, score_send, score_recv, w_send, w_recv,
    sib_send, sib_recv, z_send, z_recv,
):
    step = angles // S
    own = owned * per_block
    chips = n_dom // 2
    unit = 2 * own
    span = S2 * unit
    groups = rolled.shape[0]
    cycles = groups * G
    particles = img_ref.shape[0] // cycles
    wide = G * angles
    halves = angles // LANES
    pp = particles // n_blk
    blocks = store_ref.shape[0]
    me = lax.axis_index("dom")
    blk = lax.axis_index("blk")
    chip = me // 2
    core = me % 2
    sibling = chip * 2 + 1 - core
    far = [lax.rem(chip + o, chips) for o in range(1, chips)]
    pair = blk // 2
    blk_peers = [(1 - pair) * 2, (1 - pair) * 2 + 1, pair * 2 + 1 - blk % 2]

    barrier = pltpu.get_barrier_semaphore()
    for c in far:
        pl.semaphore_signal(barrier, inc=1, device_id={"dom": c * 2 + core}, device_id_type=MESH)
    pl.semaphore_signal(barrier, inc=1, device_id={"dom": sibling}, device_id_type=MESH)
    for b in blk_peers:
        pl.semaphore_signal(barrier, inc=1, device_id={"blk": b}, device_id_type=MESH)

    picks = [jnp.int32(0)] * owned
    seen = jnp.int32(0)
    for b in range(blocks):
        hit = (owner_ref[b] == me).astype(jnp.int32)
        for j in range(owned):
            take = jnp.logical_and(hit == 1, seen == j)
            picks[j] = jnp.where(take, jnp.int32(b), picks[j])
        seen = seen + hit
    for j in range(owned):
        block = store_ref[picks[j]].astype(jnp.float32)
        for i in range(per_block):
            k = j * per_block + i
            gain = gain_ref[picks[j] * per_block + i]
            for h in range(halves):
                blockf[h, k * cycles : (k + 1) * cycles, :] = (
                    block[i * cycles : (i + 1) * cycles, h * LANES : (h + 1) * LANES] * gain
                )
    for r in range(cycles):
        g, rr = r // G, r % G
        minef[g // 2, (g % 2) * own : (g % 2 + 1) * own, rr * angles : (rr + 1) * angles] = (
            every(blockf, r, own, cycles)
        )
    refs[me] = minef[...].astype(jnp.bfloat16)

    pl.semaphore_wait(barrier, len(far) + 1 + len(blk_peers))

    def ref_copy(slot, target, send):
        return pltpu.make_async_remote_copy(
            src_ref=refs.at[slot], dst_ref=refs.at[slot], send_sem=send,
            recv_sem=ref_recv.at[slot], device_id={"dom": target}, device_id_type=MESH,
        )

    out_copies = [ref_copy(me, c * 2 + core, ref_send.at[o]) for o, c in enumerate(far)]
    out_copies.append(ref_copy(me, sibling, ref_send.at[chips - 1]))
    for copy in out_copies:
        copy.start()

    def widen(i, carry):
        at = pl.ds(pl.multiple_of(i * 256, 256), 256)
        for h in range(halves):
            imgf[h, at, :] = img_ref[at, h * LANES : (h + 1) * LANES].astype(jnp.float32)
        return carry

    lax.fori_loop(0, particles * cycles // 256, widen, 0)

    def roll_images(g, carry):
        for rr in range(G):
            x = every(imgf, g * G + rr, particles, cycles)
            for s1 in range(S1):
                r = roll_cycles(x, step * s1, angles).astype(jnp.bfloat16)
                for j in range(n_blk):
                    at = j * pp * S1 + s1 * pp
                    rolled[g, at : at + pp, rr * angles : (rr + 1) * angles] = r[
                        j * pp : (j + 1) * pp, :
                    ]
        return carry

    lax.fori_loop(0, groups, roll_images, 0)
    lanes = pp * S1

    def score_copy(u, src, slot, target, o):
        return pltpu.make_async_remote_copy(
            src_ref=scores.at[u, src], dst_ref=got.at[u, slot], send_sem=score_send.at[u, o],
            recv_sem=score_recv.at[u, slot], device_id={"blk": target}, device_id_type=MESH,
        )

    fwd, score_copies = [], []
    for i in range(chips):
        u = lax.rem(chip + chips - i, chips)
        if i == 0:
            ref_copy(sibling, sibling, ref_send.at[chips - 1]).wait_recv()
        else:
            slot = u * 2 + core
            ref_copy(slot, slot, ref_send.at[i - 1]).wait_recv()
            copy = ref_copy(slot, sibling, fwd_send.at[i - 1])
            copy.start()
            fwd.append(copy)
            ref_copy(u * 2 + 1 - core, sibling, fwd_send.at[i - 1]).wait_recv()
        norm[...] = jnp.zeros_like(norm)
        scores[u] = jnp.zeros(scores.shape[1:], jnp.float32)

        def body(gp, carry, u=u):
            for e in range(2):
                y = refs[u * 2 + e, gp].astype(jnp.float32)
                for h in range(2):
                    flat[h, e * own : (e + 1) * own, :] = y[h * own : (h + 1) * own, :]
            for h in range(2):
                y = flat[h]
                half = 0.5 * jnp.sum(y * y, axis=1, keepdims=True)
                norm[...] += jnp.broadcast_to(half, norm.shape)
                for s2 in range(S2):
                    turned[h, s2 * unit : (s2 + 1) * unit, :] = roll_cycles(
                        y, -step * S1 * s2, angles
                    ).astype(jnp.bfloat16)
            for h in range(2):
                prod = lax.dot_general(
                    turned[h], rolled[gp * 2 + h], NT, preferred_element_type=jnp.float32
                )
                for j in range(n_blk):
                    scores[u, j] += prod[:, j * lanes : (j + 1) * lanes]
            return carry

        lax.fori_loop(0, groups // 2, body, 0)
        for j in range(n_blk):
            for s2 in range(S2):
                scores[u, j, s2 * unit : (s2 + 1) * unit, :] -= norm[...]
        copies = [score_copy(u, b, blk, b, o) for o, b in enumerate(blk_peers)]
        for o in (1, 0, 2):
            copies[o].start()
        score_copies += copies

    for u in range(chips):
        for o, b in enumerate(blk_peers):
            score_copy(u, b, b, b, o).wait_recv()
    total = jnp.concatenate(
        [
            functools.reduce(jnp.add, [got[u, b] for b in blk_peers], scores[u, blk])
            for u in range(chips)
        ],
        axis=0,
    )
    logits = total * prec_ref[blk][0:1, :]
    top = jnp.broadcast_to(jnp.max(logits, axis=0, keepdims=True), (8, lanes))
    top = spread_lanes(jnp.maximum, top, pp)[0:1, :]
    e = jnp.exp(logits - top)
    mass = jnp.broadcast_to(jnp.sum(e, axis=0, keepdims=True), (8, lanes))
    mass = spread_lanes(jnp.add, mass, pp)[0:1, :]
    weights[blk] = (e * (1.0 / mass)).astype(jnp.bfloat16)

    def w_copy(slot, target, o):
        return pltpu.make_async_remote_copy(
            src_ref=weights.at[slot], dst_ref=weights.at[slot], send_sem=w_send.at[o],
            recv_sem=w_recv.at[slot], device_id={"blk": target}, device_id_type=MESH,
        )

    w_copies = [w_copy(blk, b, o) for o, b in enumerate(blk_peers)]
    for o in (1, 0, 2):
        w_copies[o].start()
    for o, b in enumerate(blk_peers):
        w_copy(b, b, o).wait_recv()

    per_piece = groups // PIECES

    def sib_copy(q, which):
        return pltpu.make_async_remote_copy(
            src_ref=parts.at[which, q], dst_ref=sib.at[q], send_sem=sib_send.at[q],
            recv_sem=sib_recv.at[q], device_id={"dom": sibling}, device_id_type=MESH,
        )

    def z_copy(q, src, slot, target, o):
        return pltpu.make_async_remote_copy(
            src_ref=zout.at[q, src], dst_ref=zin.at[q, slot], send_sem=z_send.at[q, o],
            recv_sem=z_recv.at[q, slot], device_id={"dom": target * 2 + core}, device_id_type=MESH,
        )

    sib_copies, z_copies = [], []
    for q in range(PIECES + 1):
        if q < PIECES:

            def body(gi, carry, q=q):
                w = jnp.concatenate([weights[j] for j in range(n_blk)], axis=1)
                spread = jnp.dot(
                    w, rolled[q * per_piece + gi], preferred_element_type=jnp.float32
                )
                for u in range(chips):
                    base = u * span
                    running = spread[base + (S2 - 1) * unit : base + span, :]
                    for s2 in reversed(range(S2 - 1)):
                        running = (
                            roll_cycles(running, step * S1, angles)
                            + spread[base + s2 * unit : base + (s2 + 1) * unit, :]
                        )
                    for k in range(2):
                        d = u * 2 + k
                        parts[d % 2, q, d // 2, gi] = running[k * own : (k + 1) * own, :]
                return carry

            lax.fori_loop(0, per_piece, body, 0)
            copy = sib_copy(q, 1 - core)
            copy.start()
            sib_copies.append(copy)
        if q >= 1:
            p = q - 1
            sib_copy(p, 1 - core).wait_recv()
            for c in range(chips):
                both = parts[core, p, c] + sib[p, c]
                parts[core, p, c] = both
                zout[p, c] = both.reshape(per_piece * own, wide).astype(jnp.bfloat16)
            for o, c in enumerate(far):
                copy = z_copy(p, c, chip, c, o)
                copy.start()
                z_copies.append(copy)

    for q in range(PIECES):
        total = parts[core, q, chip].reshape(per_piece * own, wide)
        for o, c in enumerate(far):
            z_copy(q, c, c, c, o).wait_recv()
            total = total + zin[q, c].astype(jnp.float32)
        for gi in range(per_piece):
            for rr in range(G):
                out_ref[:, (q * per_piece + gi) * G + rr, :] = total[
                    gi * own : (gi + 1) * own, rr * angles : (rr + 1) * angles
                ]

    for copy in out_copies + fwd + score_copies + w_copies + sib_copies + z_copies:
        copy.wait_send()


def shards(images, ref_store, block_owner, class_gain, precision):
    particles, cycles, angles = images.shape
    n_dom = lax.axis_size("dom")
    n_blk = lax.axis_size("blk")
    blocks = block_owner.shape[0]
    per_block = ref_store.shape[2]
    owned = blocks // n_dom
    own = owned * per_block
    classes = blocks * per_block
    groups = cycles // G
    wide = G * angles
    chips = n_dom // 2
    unit = 2 * own
    pp = particles // n_blk
    lhs = S2 * classes
    rhs = S1 * particles
    per_piece = groups // PIECES

    flat_images = images.reshape(particles * cycles, angles)
    store = ref_store.reshape(blocks, per_block * cycles, angles)
    prec = jnp.tile(precision.reshape(n_blk, 1, pp), (1, 8, S1))

    vmem = pl.BlockSpec(memory_space=pltpu.VMEM)
    smem = pl.BlockSpec(memory_space=pltpu.SMEM)
    bf16, f32 = jnp.bfloat16, jnp.float32
    dma = pltpu.SemaphoreType.DMA
    out = pl.pallas_call(
        functools.partial(kernel, n_dom, n_blk, angles, per_block, owned),
        in_specs=[smem, smem, vmem, vmem, vmem],
        out_specs=vmem,
        out_shape=jax.ShapeDtypeStruct((own, cycles, angles), f32),
        scratch_shapes=[
            pltpu.VMEM((angles // LANES, particles * cycles, LANES), f32),
            pltpu.VMEM((angles // LANES, own * cycles, LANES), f32),
            pltpu.VMEM((groups // 2, 2 * own, wide), f32),
            pltpu.VMEM((n_dom, groups // 2, 2 * own, wide), bf16),
            pltpu.VMEM((groups, rhs, wide), bf16),
            pltpu.VMEM((2, S2 * unit, wide), bf16),
            pltpu.VMEM((2, unit, wide), f32),
            pltpu.VMEM((unit, pp * S1), f32),
            pltpu.VMEM((chips, n_blk, S2 * unit, pp * S1), f32),
            pltpu.VMEM((chips, n_blk, S2 * unit, pp * S1), f32),
            pltpu.VMEM((n_blk, lhs, pp * S1), bf16),
            pltpu.VMEM((2, PIECES, chips, per_piece, own, wide), f32),
            pltpu.VMEM((PIECES, chips, per_piece, own, wide), f32),
            pltpu.VMEM((PIECES, chips, per_piece * own, wide), bf16),
            pltpu.VMEM((PIECES, chips, per_piece * own, wide), bf16),
            dma((chips,)), dma((n_dom,)), dma((chips,)),
            dma((chips, n_blk)), dma((chips, n_blk)), dma((n_blk,)), dma((n_blk,)),
            dma((PIECES,)), dma((PIECES,)), dma((PIECES, chips)), dma((PIECES, chips)),
        ],
        compiler_params=pltpu.CompilerParams(
            collective_id=0, has_side_effects=True, vmem_limit_bytes=52 * 1024 * 1024
        ),
        cost_estimate=pl.CostEstimate(
            flops=4 * lhs * rhs * groups * wide, bytes_accessed=4 * 1024 * 1024, transcendentals=0
        ),
        name="fused",
    )(block_owner, class_gain, prec, flat_images, store)
    return out.reshape(1, owned, per_block, cycles, angles)


def solution(mesh):
    return jax.shard_map(
        shards,
        mesh=mesh,
        in_specs=(P("dom", "blk", None), P("dom", None, None, "blk", None), P(), P(), P("dom")),
        out_specs=P("dom", None, None, "blk", None),
        check_vma=False,
    )
```

```python
import functools
import jax
import jax.numpy as jnp
from jax import lax
from jax.experimental import pallas as pl
from jax.experimental.pallas import tpu as pltpu
from jax.sharding import PartitionSpec as P

S = 64
S1 = 8
S2 = 8
G = 4
PIECES = 4
LANES = 128
NT = (((1,), (1,)), ((), ()))
MESH = pl.DeviceIdType.MESH


def roll_cycles(x, shift, angles):
    shift = shift % angles
    if shift == 0:
        return x
    parts = [
        pltpu.roll(x[:, c * angles : (c + 1) * angles], shift, 1)
        for c in range(x.shape[1] // angles)
    ]
    return jnp.concatenate(parts, axis=1)


def swap_halves(x, angles):
    half = angles // 2
    parts = []
    for c in range(x.shape[1] // angles):
        parts.append(x[:, c * angles + half : (c + 1) * angles])
        parts.append(x[:, c * angles : c * angles + half])
    return jnp.concatenate(parts, axis=1)


def every(ref, start, count, stride):
    return jnp.concatenate(
        [ref[h, pl.ds(start, count, stride=stride), :] for h in range(ref.shape[0])], axis=1
    )


def spread_lanes(op, x, width):
    shift = width
    while shift < x.shape[1]:
        x = op(x, pltpu.roll(x, shift, 1))
        shift *= 2
    return x


def kernel(
    n_dom, n_blk, angles, per_block, owned,
    owner_ref, gain_ref, prec_ref, img_hbm, store_hbm, out_ref,
    img_ref, store_ref, imgf, blockf, minef, refs, rolled, turned, flat, norm, scores, got, weights, whole, parts, sib, zout, zin,
    ref_send, ref_recv, fwd_send, score_send, score_recv, w_send, w_recv,
    sib_send, sib_recv, z_send, z_recv, local,
):
    step = angles // S
    own = owned * per_block
    chips = n_dom // 2
    unit = 2 * own
    span = S2 * unit
    groups = rolled.shape[0]
    cycles = groups * G
    particles = img_ref.shape[0] // cycles
    wide = G * angles
    halves = angles // LANES
    pp = particles // n_blk
    blocks = store_ref.shape[0]
    me = lax.axis_index("dom")
    blk = lax.axis_index("blk")
    chip = me // 2
    core = me % 2
    sibling = chip * 2 + 1 - core
    far = [lax.rem(chip + o, chips) for o in range(1, chips)]
    pair = blk // 2
    blk_peers = [(1 - pair) * 2, (1 - pair) * 2 + 1, pair * 2 + 1 - blk % 2]

    store_in = pltpu.make_async_copy(store_hbm, store_ref, local.at[0])
    img_in = pltpu.make_async_copy(img_hbm, img_ref, local.at[1])
    store_in.start()
    img_in.start()
    barrier = pltpu.get_barrier_semaphore()
    for c in far:
        pl.semaphore_signal(barrier, inc=1, device_id={"dom": c * 2 + core}, device_id_type=MESH)
    pl.semaphore_signal(barrier, inc=1, device_id={"dom": sibling}, device_id_type=MESH)
    for b in blk_peers:
        pl.semaphore_signal(barrier, inc=1, device_id={"blk": b}, device_id_type=MESH)

    picks = [jnp.int32(0)] * owned
    seen = jnp.int32(0)
    for b in range(blocks):
        hit = (owner_ref[b] == me).astype(jnp.int32)
        for j in range(owned):
            take = jnp.logical_and(hit == 1, seen == j)
            picks[j] = jnp.where(take, jnp.int32(b), picks[j])
        seen = seen + hit
    store_in.wait()
    for j in range(owned):
        block = store_ref[picks[j]].astype(jnp.float32)
        for i in range(per_block):
            k = j * per_block + i
            gain = gain_ref[picks[j] * per_block + i]
            for h in range(halves):
                blockf[h, k * cycles : (k + 1) * cycles, :] = (
                    block[i * cycles : (i + 1) * cycles, h * LANES : (h + 1) * LANES] * gain
                )
    for r in range(cycles):
        g, rr = r // G, r % G
        minef[g // 2, (g % 2) * own : (g % 2 + 1) * own, rr * angles : (rr + 1) * angles] = (
            every(blockf, r, own, cycles)
        )
    refs[me] = minef[...].astype(jnp.bfloat16)

    pl.semaphore_wait(barrier, len(far) + 1 + len(blk_peers))

    def ref_copy(slot, target, send):
        return pltpu.make_async_remote_copy(
            src_ref=refs.at[slot], dst_ref=refs.at[slot], send_sem=send,
            recv_sem=ref_recv.at[slot], device_id={"dom": target}, device_id_type=MESH,
        )

    out_copies = [ref_copy(me, c * 2 + core, ref_send.at[o]) for o, c in enumerate(far)]
    out_copies.append(ref_copy(me, sibling, ref_send.at[chips - 1]))
    for copy in out_copies:
        copy.start()

    img_in.wait()

    def widen(i, carry):
        at = pl.ds(pl.multiple_of(i * 256, 256), 256)
        for h in range(halves):
            imgf[h, at, :] = img_ref[at, h * LANES : (h + 1) * LANES].astype(jnp.float32)
        return carry

    lax.fori_loop(0, particles * cycles // 256, widen, 0)

    def roll_images(g, carry):
        for rr in range(G):
            x = every(imgf, g * G + rr, particles, cycles).astype(jnp.bfloat16)
            for s1 in range(S1):
                r = roll_cycles(x, step * s1, angles)
                for j in range(n_blk):
                    at = j * pp * S1 + s1 * pp
                    rolled[g, at : at + pp, rr * angles : (rr + 1) * angles] = r[
                        j * pp : (j + 1) * pp, :
                    ]
        return carry

    lax.fori_loop(0, groups, roll_images, 0)
    lanes = pp * S1

    def score_copy(u, src, slot, target, o):
        return pltpu.make_async_remote_copy(
            src_ref=scores.at[u, src], dst_ref=got.at[u, slot], send_sem=score_send.at[u, o],
            recv_sem=score_recv.at[u, slot], device_id={"blk": target}, device_id_type=MESH,
        )

    fwd, score_copies = [], []
    for i in range(chips):
        u = lax.rem(chip + chips - i, chips)
        if i == 0:
            ref_copy(sibling, sibling, ref_send.at[chips - 1]).wait_recv()
        else:
            slot = u * 2 + core
            ref_copy(slot, slot, ref_send.at[i - 1]).wait_recv()
            copy = ref_copy(slot, sibling, fwd_send.at[i - 1])
            copy.start()
            fwd.append(copy)
            ref_copy(u * 2 + 1 - core, sibling, fwd_send.at[i - 1]).wait_recv()
        norm[...] = jnp.zeros_like(norm)
        scores[u] = jnp.zeros(scores.shape[1:], jnp.float32)

        def body(gp, carry, u=u):
            for e in range(2):
                y = refs[u * 2 + e, gp].astype(jnp.float32)
                for h in range(2):
                    flat[h, e * own : (e + 1) * own, :] = y[h * own : (h + 1) * own, :]
            for h in range(2):
                y = flat[h]
                half = 0.5 * jnp.sum(y * y, axis=1, keepdims=True)
                norm[...] += jnp.broadcast_to(half, norm.shape)
                y16 = y.astype(jnp.bfloat16)
                for s2 in range(S2 // 2):
                    t = roll_cycles(y16, -step * S1 * s2, angles)
                    turned[h, s2 * unit : (s2 + 1) * unit, :] = t
                    at = (s2 + S2 // 2) * unit
                    turned[h, at : at + unit, :] = swap_halves(t, angles)
            for h in range(2):
                prod = lax.dot_general(
                    turned[h], rolled[gp * 2 + h], NT, preferred_element_type=jnp.float32
                )
                for j in range(n_blk):
                    scores[u, j] += prod[:, j * lanes : (j + 1) * lanes]
            return carry

        lax.fori_loop(0, groups // 2, body, 0)
        for j in range(n_blk):
            for s2 in range(S2):
                scores[u, j, s2 * unit : (s2 + 1) * unit, :] -= norm[...]
        copies = [score_copy(u, b, blk, b, o) for o, b in enumerate(blk_peers)]
        for o in (1, 0, 2):
            copies[o].start()
        score_copies += copies

    for u in range(chips):
        for o, b in enumerate(blk_peers):
            score_copy(u, b, b, b, o).wait_recv()
    total = jnp.concatenate(
        [
            functools.reduce(jnp.add, [got[u, b] for b in blk_peers], scores[u, blk])
            for u in range(chips)
        ],
        axis=0,
    )
    lane = lax.broadcasted_iota(jnp.int32, (8, lanes), 1) & (pp - 1)
    prec = jnp.zeros((8, lanes), jnp.float32)
    for i in range(pp):
        prec = jnp.where(lane == i, prec_ref[blk * pp + i], prec)
    logits = total * prec[0:1, :]
    top = jnp.broadcast_to(jnp.max(logits, axis=0, keepdims=True), (8, lanes))
    top = spread_lanes(jnp.maximum, top, pp)[0:1, :]
    e = jnp.exp(logits - top)
    mass = jnp.broadcast_to(jnp.sum(e, axis=0, keepdims=True), (8, lanes))
    mass = spread_lanes(jnp.add, mass, pp)[0:1, :]
    weights[blk] = (e * (1.0 / mass)).astype(jnp.bfloat16)

    def w_copy(slot, target, o):
        return pltpu.make_async_remote_copy(
            src_ref=weights.at[slot], dst_ref=weights.at[slot], send_sem=w_send.at[o],
            recv_sem=w_recv.at[slot], device_id={"blk": target}, device_id_type=MESH,
        )

    w_copies = [w_copy(blk, b, o) for o, b in enumerate(blk_peers)]
    for o in (1, 0, 2):
        w_copies[o].start()
    for o, b in enumerate(blk_peers):
        w_copy(b, b, o).wait_recv()

    for j in range(n_blk):
        whole[:, j * lanes : (j + 1) * lanes] = weights[j]
    per_piece = groups // PIECES

    def sib_copy(q, which):
        return pltpu.make_async_remote_copy(
            src_ref=parts.at[which, q], dst_ref=sib.at[q], send_sem=sib_send.at[q],
            recv_sem=sib_recv.at[q], device_id={"dom": sibling}, device_id_type=MESH,
        )

    def z_copy(q, src, slot, target, o):
        return pltpu.make_async_remote_copy(
            src_ref=zout.at[q, src], dst_ref=zin.at[q, slot], send_sem=z_send.at[q, o],
            recv_sem=z_recv.at[q, slot], device_id={"dom": target * 2 + core}, device_id_type=MESH,
        )

    sib_copies, z_copies = [], []
    for q in range(PIECES + 1):
        if q < PIECES:

            def body(gi, carry, q=q):
                spread = jnp.dot(
                    whole[...], rolled[q * per_piece + gi], preferred_element_type=jnp.float32
                )
                for u in range(chips):
                    base = u * span
                    fold = [
                        spread[base + s2 * unit : base + (s2 + 1) * unit, :]
                        + swap_halves(
                            spread[base + span // 2 + s2 * unit :][:unit, :], angles
                        )
                        for s2 in range(S2 // 2)
                    ]
                    running = fold[-1]
                    for s2 in reversed(range(S2 // 2 - 1)):
                        running = roll_cycles(running, step * S1, angles) + fold[s2]
                    for k in range(2):
                        d = u * 2 + k
                        parts[d % 2, q, d // 2, gi] = running[k * own : (k + 1) * own, :]
                return carry

            lax.fori_loop(0, per_piece, body, 0)
            copy = sib_copy(q, 1 - core)
            copy.start()
            sib_copies.append(copy)
        if q >= 1:
            p = q - 1
            sib_copy(p, 1 - core).wait_recv()
            for c in range(chips):
                both = parts[core, p, c] + sib[p, c]
                parts[core, p, c] = both
                zout[p, c] = both.reshape(per_piece * own, wide).astype(jnp.bfloat16)
            for o, c in enumerate(far):
                copy = z_copy(p, c, chip, c, o)
                copy.start()
                z_copies.append(copy)

    for q in range(PIECES):
        total = parts[core, q, chip].reshape(per_piece * own, wide)
        for o, c in enumerate(far):
            z_copy(q, c, c, c, o).wait_recv()
            total = total + zin[q, c].astype(jnp.float32)
        for gi in range(per_piece):
            for rr in range(G):
                out_ref[:, (q * per_piece + gi) * G + rr, :] = total[
                    gi * own : (gi + 1) * own, rr * angles : (rr + 1) * angles
                ]

    for copy in out_copies + fwd + score_copies + w_copies + sib_copies + z_copies:
        copy.wait_send()


def shards(images, ref_store, block_owner, class_gain, precision):
    particles, cycles, angles = images.shape
    n_dom = lax.axis_size("dom")
    n_blk = lax.axis_size("blk")
    blocks = block_owner.shape[0]
    per_block = ref_store.shape[2]
    owned = blocks // n_dom
    own = owned * per_block
    classes = blocks * per_block
    groups = cycles // G
    wide = G * angles
    chips = n_dom // 2
    unit = 2 * own
    pp = particles // n_blk
    lhs = S2 * classes
    rhs = S1 * particles
    per_piece = groups // PIECES

    flat_images = images.reshape(particles * cycles, angles)
    store = ref_store.reshape(blocks, per_block * cycles, angles)

    vmem = pl.BlockSpec(memory_space=pltpu.VMEM)
    smem = pl.BlockSpec(memory_space=pltpu.SMEM)
    hbm = pl.BlockSpec(memory_space=pl.ANY)
    bf16, f32 = jnp.bfloat16, jnp.float32
    dma = pltpu.SemaphoreType.DMA
    out = pl.pallas_call(
        functools.partial(kernel, n_dom, n_blk, angles, per_block, owned),
        in_specs=[smem, smem, smem, hbm, hbm],
        out_specs=vmem,
        out_shape=jax.ShapeDtypeStruct((own, cycles, angles), f32),
        scratch_shapes=[
            pltpu.VMEM((particles * cycles, angles), bf16),
            pltpu.VMEM((blocks, per_block * cycles, angles), bf16),
            pltpu.VMEM((angles // LANES, particles * cycles, LANES), f32),
            pltpu.VMEM((angles // LANES, own * cycles, LANES), f32),
            pltpu.VMEM((groups // 2, 2 * own, wide), f32),
            pltpu.VMEM((n_dom, groups // 2, 2 * own, wide), bf16),
            pltpu.VMEM((groups, rhs, wide), bf16),
            pltpu.VMEM((2, S2 * unit, wide), bf16),
            pltpu.VMEM((2, unit, wide), f32),
            pltpu.VMEM((unit, pp * S1), f32),
            pltpu.VMEM((chips, n_blk, S2 * unit, pp * S1), f32),
            pltpu.VMEM((chips, n_blk, S2 * unit, pp * S1), f32),
            pltpu.VMEM((n_blk, lhs, pp * S1), bf16),
            pltpu.VMEM((lhs, rhs), bf16),
            pltpu.VMEM((2, PIECES, chips, per_piece, own, wide), f32),
            pltpu.VMEM((PIECES, chips, per_piece, own, wide), f32),
            pltpu.VMEM((PIECES, chips, per_piece * own, wide), bf16),
            pltpu.VMEM((PIECES, chips, per_piece * own, wide), bf16),
            dma((chips,)), dma((n_dom,)), dma((chips,)),
            dma((chips, n_blk)), dma((chips, n_blk)), dma((n_blk,)), dma((n_blk,)),
            dma((PIECES,)), dma((PIECES,)), dma((PIECES, chips)), dma((PIECES, chips)), dma((2,)),
        ],
        compiler_params=pltpu.CompilerParams(
            collective_id=0, has_side_effects=True, vmem_limit_bytes=52 * 1024 * 1024
        ),
        cost_estimate=pl.CostEstimate(
            flops=4 * lhs * rhs * groups * wide, bytes_accessed=4 * 1024 * 1024, transcendentals=0
        ),
        name="fused",
    )(block_owner, class_gain, precision, flat_images, store)
    return out.reshape(1, owned, per_block, cycles, angles)


def solution(mesh):
    return jax.shard_map(
        shards,
        mesh=mesh,
        in_specs=(P("dom", "blk", None), P("dom", None, None, "blk", None), P(), P(), P("dom")),
        out_specs=P("dom", None, None, "blk", None),
        check_vma=False,
    )
```

```python
import functools
import jax
import jax.numpy as jnp
from jax import lax
from jax.experimental import pallas as pl
from jax.experimental.pallas import tpu as pltpu
from jax.sharding import PartitionSpec as P

S = 64
S1 = 8
S2 = 8
G = 4
PIECES = 4
LANES = 128
NT = (((1,), (1,)), ((), ()))
MESH = pl.DeviceIdType.MESH


def roll_cycles(x, shift, angles):
    shift = shift % angles
    if shift == 0:
        return x
    parts = [
        pltpu.roll(x[:, c * angles : (c + 1) * angles], shift, 1)
        for c in range(x.shape[1] // angles)
    ]
    return jnp.concatenate(parts, axis=1)


def swap_halves(x, angles):
    half = angles // 2
    parts = []
    for c in range(x.shape[1] // angles):
        parts.append(x[:, c * angles + half : (c + 1) * angles])
        parts.append(x[:, c * angles : c * angles + half])
    return jnp.concatenate(parts, axis=1)


def every(ref, start, count, stride):
    return jnp.concatenate(
        [ref[h, pl.ds(start, count, stride=stride), :] for h in range(ref.shape[0])], axis=1
    )


def spread_lanes(op, x, width):
    shift = width
    while shift < x.shape[1]:
        x = op(x, pltpu.roll(x, shift, 1))
        shift *= 2
    return x


def kernel(
    n_dom, n_blk, angles, per_block, owned,
    owner_hbm, gain_hbm, prec_hbm, img_hbm, store_hbm, out_ref,
    owner_ref, gain_ref, prec_ref, img_ref, store_ref, imgf, blockf, minef, refs, rolled, turned, flat, norm, scores, got, weights, whole, parts, sib, zout, zin,
    ref_send, ref_recv, fwd_send, score_send, score_recv, w_send, w_recv,
    sib_send, sib_recv, z_send, z_recv, local,
):
    step = angles // S
    own = owned * per_block
    chips = n_dom // 2
    unit = 2 * own
    span = S2 * unit
    groups = rolled.shape[0]
    cycles = groups * G
    particles = img_ref.shape[0] // cycles
    wide = G * angles
    halves = angles // LANES
    pp = particles // n_blk
    blocks = store_ref.shape[0]
    me = lax.axis_index("dom")
    blk = lax.axis_index("blk")
    chip = me // 2
    core = me % 2
    sibling = chip * 2 + 1 - core
    far = [lax.rem(chip + o, chips) for o in range(1, chips)]
    pair = blk // 2
    blk_peers = [(1 - pair) * 2, (1 - pair) * 2 + 1, pair * 2 + 1 - blk % 2]

    store_in = pltpu.make_async_copy(store_hbm, store_ref, local.at[0])
    img_in = pltpu.make_async_copy(img_hbm, img_ref, local.at[1])
    small_in = [
        pltpu.make_async_copy(owner_hbm, owner_ref, local.at[2]),
        pltpu.make_async_copy(gain_hbm, gain_ref, local.at[3]),
        pltpu.make_async_copy(prec_hbm, prec_ref, local.at[4]),
    ]
    for copy in small_in:
        copy.start()
    store_in.start()
    img_in.start()
    barrier = pltpu.get_barrier_semaphore()
    for c in far:
        pl.semaphore_signal(barrier, inc=1, device_id={"dom": c * 2 + core}, device_id_type=MESH)
    pl.semaphore_signal(barrier, inc=1, device_id={"dom": sibling}, device_id_type=MESH)
    for b in blk_peers:
        pl.semaphore_signal(barrier, inc=1, device_id={"blk": b}, device_id_type=MESH)

    for copy in small_in:
        copy.wait()
    picks = [jnp.int32(0)] * owned
    seen = jnp.int32(0)
    for b in range(blocks):
        hit = (owner_ref[b] == me).astype(jnp.int32)
        for j in range(owned):
            take = jnp.logical_and(hit == 1, seen == j)
            picks[j] = jnp.where(take, jnp.int32(b), picks[j])
        seen = seen + hit
    store_in.wait()
    for j in range(owned):
        block = store_ref[picks[j]].astype(jnp.float32)
        for i in range(per_block):
            k = j * per_block + i
            gain = gain_ref[picks[j] * per_block + i]
            for h in range(halves):
                blockf[h, k * cycles : (k + 1) * cycles, :] = (
                    block[i * cycles : (i + 1) * cycles, h * LANES : (h + 1) * LANES] * gain
                )
    for r in range(cycles):
        g, rr = r // G, r % G
        minef[g // 2, (g % 2) * own : (g % 2 + 1) * own, rr * angles : (rr + 1) * angles] = (
            every(blockf, r, own, cycles)
        )
    refs[me] = minef[...].astype(jnp.bfloat16)

    pl.semaphore_wait(barrier, len(far) + 1 + len(blk_peers))

    def ref_copy(slot, target, send):
        return pltpu.make_async_remote_copy(
            src_ref=refs.at[slot], dst_ref=refs.at[slot], send_sem=send,
            recv_sem=ref_recv.at[slot], device_id={"dom": target}, device_id_type=MESH,
        )

    out_copies = [ref_copy(me, c * 2 + core, ref_send.at[o]) for o, c in enumerate(far)]
    out_copies.append(ref_copy(me, sibling, ref_send.at[chips - 1]))
    for copy in out_copies:
        copy.start()

    img_in.wait()

    def widen(i, carry):
        at = pl.ds(pl.multiple_of(i * 256, 256), 256)
        for h in range(halves):
            imgf[h, at, :] = img_ref[at, h * LANES : (h + 1) * LANES].astype(jnp.float32)
        return carry

    lax.fori_loop(0, particles * cycles // 256, widen, 0)

    def roll_images(g, carry):
        for rr in range(G):
            x = every(imgf, g * G + rr, particles, cycles).astype(jnp.bfloat16)
            for s1 in range(S1):
                r = roll_cycles(x, step * s1, angles)
                for j in range(n_blk):
                    at = j * pp * S1 + s1 * pp
                    rolled[g, at : at + pp, rr * angles : (rr + 1) * angles] = r[
                        j * pp : (j + 1) * pp, :
                    ]
        return carry

    lax.fori_loop(0, groups, roll_images, 0)
    lanes = pp * S1

    def score_copy(u, src, slot, target, o):
        return pltpu.make_async_remote_copy(
            src_ref=scores.at[u, src], dst_ref=got.at[u, slot], send_sem=score_send.at[u, o],
            recv_sem=score_recv.at[u, slot], device_id={"blk": target}, device_id_type=MESH,
        )

    fwd, score_copies = [], []
    for i in range(chips):
        u = lax.rem(chip + chips - i, chips)
        if i == 0:
            ref_copy(sibling, sibling, ref_send.at[chips - 1]).wait_recv()
        else:
            slot = u * 2 + core
            ref_copy(slot, slot, ref_send.at[i - 1]).wait_recv()
            copy = ref_copy(slot, sibling, fwd_send.at[i - 1])
            copy.start()
            fwd.append(copy)
            ref_copy(u * 2 + 1 - core, sibling, fwd_send.at[i - 1]).wait_recv()
        norm[...] = jnp.zeros_like(norm)
        scores[u] = jnp.zeros(scores.shape[1:], jnp.float32)

        def body(gp, carry, u=u):
            for e in range(2):
                y = refs[u * 2 + e, gp].astype(jnp.float32)
                for h in range(2):
                    flat[h, e * own : (e + 1) * own, :] = y[h * own : (h + 1) * own, :]
            for h in range(2):
                y = flat[h]
                half = 0.5 * jnp.sum(y * y, axis=1, keepdims=True)
                norm[...] += jnp.broadcast_to(half, norm.shape)
                y16 = y.astype(jnp.bfloat16)
                for s2 in range(S2 // 2):
                    t = roll_cycles(y16, -step * S1 * s2, angles)
                    turned[h, s2 * unit : (s2 + 1) * unit, :] = t
                    at = (s2 + S2 // 2) * unit
                    turned[h, at : at + unit, :] = swap_halves(t, angles)
            for h in range(2):
                prod = lax.dot_general(
                    turned[h], rolled[gp * 2 + h], NT, preferred_element_type=jnp.float32
                )
                for j in range(n_blk):
                    scores[u, j] += prod[:, j * lanes : (j + 1) * lanes]
            return carry

        lax.fori_loop(0, groups // 2, body, 0)
        for j in range(n_blk):
            for s2 in range(S2):
                scores[u, j, s2 * unit : (s2 + 1) * unit, :] -= norm[...]
        copies = [score_copy(u, b, blk, b, o) for o, b in enumerate(blk_peers)]
        for o in (1, 0, 2):
            copies[o].start()
        score_copies += copies

    for u in range(chips):
        for o, b in enumerate(blk_peers):
            score_copy(u, b, b, b, o).wait_recv()
    total = jnp.concatenate(
        [
            functools.reduce(jnp.add, [got[u, b] for b in blk_peers], scores[u, blk])
            for u in range(chips)
        ],
        axis=0,
    )
    lane = lax.broadcasted_iota(jnp.int32, (8, lanes), 1) & (pp - 1)
    prec = jnp.zeros((8, lanes), jnp.float32)
    for i in range(pp):
        prec = jnp.where(lane == i, prec_ref[blk * pp + i], prec)
    logits = total * prec[0:1, :]
    top = jnp.broadcast_to(jnp.max(logits, axis=0, keepdims=True), (8, lanes))
    top = spread_lanes(jnp.maximum, top, pp)[0:1, :]
    e = jnp.exp(logits - top)
    mass = jnp.broadcast_to(jnp.sum(e, axis=0, keepdims=True), (8, lanes))
    mass = spread_lanes(jnp.add, mass, pp)[0:1, :]
    w = (e * (1.0 / mass)).astype(jnp.bfloat16)
    for u in range(chips):
        weights[u, blk] = w[u * span : (u + 1) * span, :]

    def w_copy(u, slot, target, o):
        return pltpu.make_async_remote_copy(
            src_ref=weights.at[u, slot], dst_ref=weights.at[u, slot], send_sem=w_send.at[u, o],
            recv_sem=w_recv.at[u, slot], device_id={"blk": target}, device_id_type=MESH,
        )

    order = far + [chip]
    w_copies = []
    for u in order:
        copies = [w_copy(u, blk, b, o) for o, b in enumerate(blk_peers)]
        for o in (1, 0, 2):
            copies[o].start()
        w_copies += copies

    per_piece = groups // PIECES
    part = chips // 2

    def sib_copy(h, q, which):
        return pltpu.make_async_remote_copy(
            src_ref=parts.at[which, h, q], dst_ref=sib.at[h, q], send_sem=sib_send.at[h, q],
            recv_sem=sib_recv.at[h, q], device_id={"dom": sibling}, device_id_type=MESH,
        )

    def z_copy(q, src, slot, target):
        return pltpu.make_async_remote_copy(
            src_ref=zout.at[q, src], dst_ref=zin.at[q, slot], send_sem=z_send.at[q, src],
            recv_sem=z_recv.at[q, slot], device_id={"dom": target * 2 + core}, device_id_type=MESH,
        )

    sib_copies, z_copies = [], []

    def finish(h, q):
        sib_copy(h, q, 1 - core).wait_recv()
        for i in range(part):
            at = h * part + i
            both = parts[core, h, q, i] + sib[h, q, i]
            if at == chips - 1:
                parts[core, h, q, i] = both
                continue
            zout[q, at] = both.reshape(per_piece * own, wide).astype(jnp.bfloat16)
            copy = z_copy(q, at, chip, order[at])
            copy.start()
            z_copies.append(copy)

    last = None
    for h in range(2):
        for i in range(part):
            u = order[h * part + i]
            for o, b in enumerate(blk_peers):
                w_copy(u, b, b, o).wait_recv()
            for j in range(n_blk):
                whole[i * span : (i + 1) * span, j * lanes : (j + 1) * lanes] = weights[u, j]
        for q in range(PIECES):

            def body(gi, carry, h=h, q=q):
                spread = jnp.dot(
                    whole[...], rolled[q * per_piece + gi], preferred_element_type=jnp.float32
                )
                for i in range(part):
                    base = i * span
                    fold = [
                        spread[base + s2 * unit : base + (s2 + 1) * unit, :]
                        + swap_halves(
                            spread[base + span // 2 + s2 * unit :][:unit, :], angles
                        )
                        for s2 in range(S2 // 2)
                    ]
                    running = fold[-1]
                    for s2 in reversed(range(S2 // 2 - 1)):
                        running = roll_cycles(running, step * S1, angles) + fold[s2]
                    for k in range(2):
                        parts[k, h, q, i, gi] = running[k * own : (k + 1) * own, :]
                return carry

            lax.fori_loop(0, per_piece, body, 0)
            copy = sib_copy(h, q, 1 - core)
            copy.start()
            sib_copies.append(copy)
            if last is not None:
                finish(*last)
            last = (h, q)
    finish(*last)

    for q in range(PIECES):
        total = parts[core, 1, q, part - 1].reshape(per_piece * own, wide)
        for c in far:
            z_copy(q, 0, c, c).wait_recv()
            total = total + zin[q, c].astype(jnp.float32)
        for gi in range(per_piece):
            for rr in range(G):
                out_ref[:, (q * per_piece + gi) * G + rr, :] = total[
                    gi * own : (gi + 1) * own, rr * angles : (rr + 1) * angles
                ]

    for copy in out_copies + fwd + score_copies + w_copies + sib_copies + z_copies:
        copy.wait_send()


def shards(images, ref_store, block_owner, class_gain, precision):
    particles, cycles, angles = images.shape
    n_dom = lax.axis_size("dom")
    n_blk = lax.axis_size("blk")
    blocks = block_owner.shape[0]
    per_block = ref_store.shape[2]
    owned = blocks // n_dom
    own = owned * per_block
    classes = blocks * per_block
    groups = cycles // G
    wide = G * angles
    chips = n_dom // 2
    unit = 2 * own
    pp = particles // n_blk
    lhs = S2 * classes
    rhs = S1 * particles
    per_piece = groups // PIECES

    flat_images = images.reshape(particles * cycles, angles)
    store = ref_store.reshape(blocks, per_block * cycles, angles)

    vmem = pl.BlockSpec(memory_space=pltpu.VMEM)
    hbm = pl.BlockSpec(memory_space=pl.ANY)
    bf16, f32 = jnp.bfloat16, jnp.float32
    dma = pltpu.SemaphoreType.DMA
    out = pl.pallas_call(
        functools.partial(kernel, n_dom, n_blk, angles, per_block, owned),
        in_specs=[hbm] * 5,
        out_specs=vmem,
        out_shape=jax.ShapeDtypeStruct((own, cycles, angles), f32),
        scratch_shapes=[
            pltpu.SMEM((blocks,), jnp.int32),
            pltpu.SMEM((classes,), f32),
            pltpu.SMEM((particles,), f32),
            pltpu.VMEM((particles * cycles, angles), bf16),
            pltpu.VMEM((blocks, per_block * cycles, angles), bf16),
            pltpu.VMEM((angles // LANES, particles * cycles, LANES), f32),
            pltpu.VMEM((angles // LANES, own * cycles, LANES), f32),
            pltpu.VMEM((groups // 2, 2 * own, wide), f32),
            pltpu.VMEM((n_dom, groups // 2, 2 * own, wide), bf16),
            pltpu.VMEM((groups, rhs, wide), bf16),
            pltpu.VMEM((2, S2 * unit, wide), bf16),
            pltpu.VMEM((2, unit, wide), f32),
            pltpu.VMEM((unit, pp * S1), f32),
            pltpu.VMEM((chips, n_blk, S2 * unit, pp * S1), f32),
            pltpu.VMEM((chips, n_blk, S2 * unit, pp * S1), f32),
            pltpu.VMEM((chips, n_blk, S2 * unit, pp * S1), bf16),
            pltpu.VMEM((lhs // 2, rhs), bf16),
            pltpu.VMEM((2, 2, PIECES, chips // 2, per_piece, own, wide), f32),
            pltpu.VMEM((2, PIECES, chips // 2, per_piece, own, wide), f32),
            pltpu.VMEM((PIECES, chips, per_piece * own, wide), bf16),
            pltpu.VMEM((PIECES, chips, per_piece * own, wide), bf16),
            dma((chips,)), dma((n_dom,)), dma((chips,)),
            dma((chips, n_blk)), dma((chips, n_blk)), dma((chips, n_blk)), dma((chips, n_blk)),
            dma((2, PIECES)), dma((2, PIECES)), dma((PIECES, chips)), dma((PIECES, chips)), dma((5,)),
        ],
        compiler_params=pltpu.CompilerParams(
            collective_id=0, has_side_effects=True, vmem_limit_bytes=60 * 1024 * 1024
        ),
        cost_estimate=pl.CostEstimate(
            flops=4 * lhs * rhs * groups * wide, bytes_accessed=4 * 1024 * 1024, transcendentals=0
        ),
        name="fused",
    )(block_owner, class_gain, precision, flat_images, store)
    return out.reshape(1, owned, per_block, cycles, angles)


def solution(mesh):
    return jax.shard_map(
        shards,
        mesh=mesh,
        in_specs=(P("dom", "blk", None), P("dom", None, None, "blk", None), P(), P(), P("dom")),
        out_specs=P("dom", None, None, "blk", None),
        check_vma=False,
    )
```

```python
import functools
import jax
import jax.numpy as jnp
from jax import lax
from jax.experimental import pallas as pl
from jax.experimental.pallas import tpu as pltpu
from jax.sharding import PartitionSpec as P

S = 64
S1 = 8
S2 = 8
G = 4
PIECES = 4
LANES = 128
NT = (((1,), (1,)), ((), ()))
MESH = pl.DeviceIdType.MESH


def roll_cycles(x, shift, angles):
    shift = shift % angles
    if shift == 0:
        return x
    parts = [
        pltpu.roll(x[:, c * angles : (c + 1) * angles], shift, 1)
        for c in range(x.shape[1] // angles)
    ]
    return jnp.concatenate(parts, axis=1)


def swap_halves(x, angles):
    half = angles // 2
    parts = []
    for c in range(x.shape[1] // angles):
        parts.append(x[:, c * angles + half : (c + 1) * angles])
        parts.append(x[:, c * angles : c * angles + half])
    return jnp.concatenate(parts, axis=1)


def every(ref, start, count, stride):
    return jnp.concatenate(
        [ref[h, pl.ds(start, count, stride=stride), :] for h in range(ref.shape[0])], axis=1
    )


def spread_lanes(op, x, width):
    shift = width
    while shift < x.shape[1]:
        x = op(x, pltpu.roll(x, shift, 1))
        shift *= 2
    return x


def kernel(
    n_dom, n_blk, angles, per_block, owned,
    owner_hbm, gain_hbm, prec_hbm, img_hbm, store_hbm, out_ref,
    owner_ref, gain_ref, prec_ref, img_ref, store_ref, imgf, blockf, minef, refs, rolled, turned, flat, norm, scores, got, weights, whole, parts, sib, zout, zin,
    ref_send, ref_recv, fwd_send, score_send, score_recv, w_send, w_recv,
    sib_send, sib_recv, z_send, z_recv, local,
):
    step = angles // S
    own = owned * per_block
    chips = n_dom // 2
    unit = 2 * own
    span = S2 * unit
    groups = rolled.shape[0]
    cycles = groups * G
    particles = img_ref.shape[0] // cycles
    wide = G * angles
    halves = angles // LANES
    pp = particles // n_blk
    blocks = store_ref.shape[0]
    me = lax.axis_index("dom")
    blk = lax.axis_index("blk")
    chip = me // 2
    core = me % 2
    sibling = chip * 2 + 1 - core
    far = [lax.rem(chip + o, chips) for o in range(1, chips)]
    pair = blk // 2
    blk_peers = [(1 - pair) * 2, (1 - pair) * 2 + 1, pair * 2 + 1 - blk % 2]

    store_in = pltpu.make_async_copy(store_hbm, store_ref, local.at[0])
    img_in = pltpu.make_async_copy(img_hbm, img_ref, local.at[1])
    small_in = [
        pltpu.make_async_copy(owner_hbm, owner_ref, local.at[2]),
        pltpu.make_async_copy(gain_hbm, gain_ref, local.at[3]),
        pltpu.make_async_copy(prec_hbm, prec_ref, local.at[4]),
    ]
    for copy in small_in:
        copy.start()
    store_in.start()
    img_in.start()
    barrier = pltpu.get_barrier_semaphore()
    for c in far:
        pl.semaphore_signal(barrier, inc=1, device_id={"dom": c * 2 + core}, device_id_type=MESH)
    pl.semaphore_signal(barrier, inc=1, device_id={"dom": sibling}, device_id_type=MESH)
    for b in blk_peers:
        pl.semaphore_signal(barrier, inc=1, device_id={"blk": b}, device_id_type=MESH)

    for copy in small_in:
        copy.wait()
    picks = [jnp.int32(0)] * owned
    seen = jnp.int32(0)
    for b in range(blocks):
        hit = (owner_ref[b] == me).astype(jnp.int32)
        for j in range(owned):
            take = jnp.logical_and(hit == 1, seen == j)
            picks[j] = jnp.where(take, jnp.int32(b), picks[j])
        seen = seen + hit
    store_in.wait()
    for j in range(owned):
        block = store_ref[picks[j]].astype(jnp.float32)
        for i in range(per_block):
            k = j * per_block + i
            gain = gain_ref[picks[j] * per_block + i]
            for h in range(halves):
                blockf[h, k * cycles : (k + 1) * cycles, :] = (
                    block[i * cycles : (i + 1) * cycles, h * LANES : (h + 1) * LANES] * gain
                )
    for r in range(cycles):
        g, rr = r // G, r % G
        minef[g // 2, (g % 2) * own : (g % 2 + 1) * own, rr * angles : (rr + 1) * angles] = (
            every(blockf, r, own, cycles)
        )
    refs[me] = minef[...].astype(jnp.bfloat16)

    pl.semaphore_wait(barrier, len(far) + 1 + len(blk_peers))

    def ref_copy(slot, target, send):
        return pltpu.make_async_remote_copy(
            src_ref=refs.at[slot], dst_ref=refs.at[slot], send_sem=send,
            recv_sem=ref_recv.at[slot], device_id={"dom": target}, device_id_type=MESH,
        )

    out_copies = [ref_copy(me, c * 2 + core, ref_send.at[o]) for o, c in enumerate(far)]
    out_copies.append(ref_copy(me, sibling, ref_send.at[chips - 1]))
    for copy in out_copies:
        copy.start()

    img_in.wait()

    def widen(i, carry):
        at = pl.ds(pl.multiple_of(i * 256, 256), 256)
        for h in range(halves):
            imgf[h, at, :] = img_ref[at, h * LANES : (h + 1) * LANES].astype(jnp.float32)
        return carry

    lax.fori_loop(0, particles * cycles // 256, widen, 0)

    def roll_images(g, carry):
        for rr in range(G):
            x = every(imgf, g * G + rr, particles, cycles).astype(jnp.bfloat16)
            for s1 in range(S1):
                r = roll_cycles(x, step * s1, angles)
                for j in range(n_blk):
                    at = j * pp * S1 + s1 * pp
                    rolled[g, at : at + pp, rr * angles : (rr + 1) * angles] = r[
                        j * pp : (j + 1) * pp, :
                    ]
        return carry

    lax.fori_loop(0, groups, roll_images, 0)
    lanes = pp * S1

    def score_copy(u, src, slot, target, o):
        return pltpu.make_async_remote_copy(
            src_ref=scores.at[u, src], dst_ref=got.at[u, slot], send_sem=score_send.at[u, o],
            recv_sem=score_recv.at[u, slot], device_id={"blk": target}, device_id_type=MESH,
        )

    fwd, score_copies = [], []
    for i in range(chips):
        u = lax.rem(chip + chips - i, chips)
        if i == 0:
            ref_copy(sibling, sibling, ref_send.at[chips - 1]).wait_recv()
        else:
            ref_copy(u * 2 + 1 - core, sibling, fwd_send.at[i - 1]).wait_recv()
        norm[...] = jnp.zeros_like(norm)
        scores[u] = jnp.zeros(scores.shape[1:], jnp.float32)

        def body(gp, carry, u=u):
            for e in range(2):
                y = refs[u * 2 + e, gp].astype(jnp.float32)
                for h in range(2):
                    flat[h, e * own : (e + 1) * own, :] = y[h * own : (h + 1) * own, :]
            for h in range(2):
                y = flat[h]
                half = 0.5 * jnp.sum(y * y, axis=1, keepdims=True)
                norm[...] += jnp.broadcast_to(half, norm.shape)
                y16 = y.astype(jnp.bfloat16)
                for s2 in range(S2 // 2):
                    t = roll_cycles(y16, -step * S1 * s2, angles)
                    turned[h, s2 * unit : (s2 + 1) * unit, :] = t
                    at = (s2 + S2 // 2) * unit
                    turned[h, at : at + unit, :] = swap_halves(t, angles)
            prod = lax.dot_general(
                turned[0], rolled[gp * 2], NT, preferred_element_type=jnp.float32
            ) + lax.dot_general(
                turned[1], rolled[gp * 2 + 1], NT, preferred_element_type=jnp.float32
            )
            for j in range(n_blk):
                scores[u, j] += prod[:, j * lanes : (j + 1) * lanes]
            return carry

        lax.fori_loop(0, groups // 4, body, 0)
        if i < chips - 1:
            slot = lax.rem(chip + chips - i - 1, chips) * 2 + core
            ref_copy(slot, slot, ref_send.at[i]).wait_recv()
            copy = ref_copy(slot, sibling, fwd_send.at[i])
            copy.start()
            fwd.append(copy)
        lax.fori_loop(groups // 4, groups // 2, body, 0)
        for j in range(n_blk):
            for s2 in range(S2):
                scores[u, j, s2 * unit : (s2 + 1) * unit, :] -= norm[...]
        copies = [score_copy(u, b, blk, b, o) for o, b in enumerate(blk_peers)]
        for o in (1, 0, 2):
            copies[o].start()
        score_copies += copies

    for u in range(chips):
        for o, b in enumerate(blk_peers):
            score_copy(u, b, b, b, o).wait_recv()
    total = jnp.concatenate(
        [
            functools.reduce(jnp.add, [got[u, b] for b in blk_peers], scores[u, blk])
            for u in range(chips)
        ],
        axis=0,
    )
    lane = lax.broadcasted_iota(jnp.int32, (8, lanes), 1) & (pp - 1)
    prec = jnp.zeros((8, lanes), jnp.float32)
    for i in range(pp):
        prec = jnp.where(lane == i, prec_ref[blk * pp + i], prec)
    logits = total * prec[0:1, :]
    top = jnp.broadcast_to(jnp.max(logits, axis=0, keepdims=True), (8, lanes))
    top = spread_lanes(jnp.maximum, top, pp)[0:1, :]
    e = jnp.exp(logits - top)
    mass = jnp.broadcast_to(jnp.sum(e, axis=0, keepdims=True), (8, lanes))
    mass = spread_lanes(jnp.add, mass, pp)[0:1, :]
    w = (e * (1.0 / mass)).astype(jnp.bfloat16)
    for u in range(chips):
        weights[u, blk] = w[u * span : (u + 1) * span, :]

    def w_copy(u, slot, target, o):
        return pltpu.make_async_remote_copy(
            src_ref=weights.at[u, slot], dst_ref=weights.at[u, slot], send_sem=w_send.at[u, o],
            recv_sem=w_recv.at[u, slot], device_id={"blk": target}, device_id_type=MESH,
        )

    order = far + [chip]
    w_copies = []
    for u in order:
        copies = [w_copy(u, blk, b, o) for o, b in enumerate(blk_peers)]
        for o in (1, 0, 2):
            copies[o].start()
        w_copies += copies

    per_piece = groups // PIECES
    part = chips // 2

    def sib_copy(h, q, which):
        return pltpu.make_async_remote_copy(
            src_ref=parts.at[which, h, q], dst_ref=sib.at[h, q], send_sem=sib_send.at[h, q],
            recv_sem=sib_recv.at[h, q], device_id={"dom": sibling}, device_id_type=MESH,
        )

    def z_copy(q, src, slot, target):
        return pltpu.make_async_remote_copy(
            src_ref=zout.at[q, src], dst_ref=zin.at[q, slot], send_sem=z_send.at[q, src],
            recv_sem=z_recv.at[q, slot], device_id={"dom": target * 2 + core}, device_id_type=MESH,
        )

    sib_copies, z_copies = [], []

    def finish(h, q):
        sib_copy(h, q, 1 - core).wait_recv()
        for i in range(part):
            at = h * part + i
            both = parts[core, h, q, i] + sib[h, q, i]
            if at == chips - 1:
                parts[core, h, q, i] = both
                continue
            zout[q, at] = both.reshape(per_piece * own, wide).astype(jnp.bfloat16)
            copy = z_copy(q, at, chip, order[at])
            copy.start()
            z_copies.append(copy)

    last = None
    for h in range(2):
        for i in range(part):
            u = order[h * part + i]
            for o, b in enumerate(blk_peers):
                w_copy(u, b, b, o).wait_recv()
            for j in range(n_blk):
                whole[i * span : (i + 1) * span, j * lanes : (j + 1) * lanes] = weights[u, j]
        for q in range(PIECES):

            def body(gi, carry, h=h, q=q):
                spread = jnp.dot(
                    whole[...], rolled[q * per_piece + gi], preferred_element_type=jnp.float32
                )
                for i in range(part):
                    base = i * span
                    fold = [
                        spread[base + s2 * unit : base + (s2 + 1) * unit, :]
                        + swap_halves(
                            spread[base + span // 2 + s2 * unit :][:unit, :], angles
                        )
                        for s2 in range(S2 // 2)
                    ]
                    running = fold[-1]
                    for s2 in reversed(range(S2 // 2 - 1)):
                        running = roll_cycles(running, step * S1, angles) + fold[s2]
                    for k in range(2):
                        parts[k, h, q, i, gi] = running[k * own : (k + 1) * own, :]
                return carry

            lax.fori_loop(0, per_piece, body, 0)
            copy = sib_copy(h, q, 1 - core)
            copy.start()
            sib_copies.append(copy)
            if last is not None:
                finish(*last)
            last = (h, q)
    finish(*last)

    for q in range(PIECES):
        total = parts[core, 1, q, part - 1].reshape(per_piece * own, wide)
        for c in far:
            z_copy(q, 0, c, c).wait_recv()
            total = total + zin[q, c].astype(jnp.float32)
        for gi in range(per_piece):
            for rr in range(G):
                out_ref[:, (q * per_piece + gi) * G + rr, :] = total[
                    gi * own : (gi + 1) * own, rr * angles : (rr + 1) * angles
                ]

    for copy in out_copies + fwd + score_copies + w_copies + sib_copies + z_copies:
        copy.wait_send()


def shards(images, ref_store, block_owner, class_gain, precision):
    particles, cycles, angles = images.shape
    n_dom = lax.axis_size("dom")
    n_blk = lax.axis_size("blk")
    blocks = block_owner.shape[0]
    per_block = ref_store.shape[2]
    owned = blocks // n_dom
    own = owned * per_block
    classes = blocks * per_block
    groups = cycles // G
    wide = G * angles
    chips = n_dom // 2
    unit = 2 * own
    pp = particles // n_blk
    lhs = S2 * classes
    rhs = S1 * particles
    per_piece = groups // PIECES

    flat_images = images.reshape(particles * cycles, angles)
    store = ref_store.reshape(blocks, per_block * cycles, angles)

    vmem = pl.BlockSpec(memory_space=pltpu.VMEM)
    hbm = pl.BlockSpec(memory_space=pl.ANY)
    bf16, f32 = jnp.bfloat16, jnp.float32
    dma = pltpu.SemaphoreType.DMA
    out = pl.pallas_call(
        functools.partial(kernel, n_dom, n_blk, angles, per_block, owned),
        in_specs=[hbm] * 5,
        out_specs=vmem,
        out_shape=jax.ShapeDtypeStruct((own, cycles, angles), f32),
        scratch_shapes=[
            pltpu.SMEM((blocks,), jnp.int32),
            pltpu.SMEM((classes,), f32),
            pltpu.SMEM((particles,), f32),
            pltpu.VMEM((particles * cycles, angles), bf16),
            pltpu.VMEM((blocks, per_block * cycles, angles), bf16),
            pltpu.VMEM((angles // LANES, particles * cycles, LANES), f32),
            pltpu.VMEM((angles // LANES, own * cycles, LANES), f32),
            pltpu.VMEM((groups // 2, 2 * own, wide), f32),
            pltpu.VMEM((n_dom, groups // 2, 2 * own, wide), bf16),
            pltpu.VMEM((groups, rhs, wide), bf16),
            pltpu.VMEM((2, S2 * unit, wide), bf16),
            pltpu.VMEM((2, unit, wide), f32),
            pltpu.VMEM((unit, pp * S1), f32),
            pltpu.VMEM((chips, n_blk, S2 * unit, pp * S1), f32),
            pltpu.VMEM((chips, n_blk, S2 * unit, pp * S1), f32),
            pltpu.VMEM((chips, n_blk, S2 * unit, pp * S1), bf16),
            pltpu.VMEM((lhs // 2, rhs), bf16),
            pltpu.VMEM((2, 2, PIECES, chips // 2, per_piece, own, wide), f32),
            pltpu.VMEM((2, PIECES, chips // 2, per_piece, own, wide), f32),
            pltpu.VMEM((PIECES, chips, per_piece * own, wide), bf16),
            pltpu.VMEM((PIECES, chips, per_piece * own, wide), bf16),
            dma((chips,)), dma((n_dom,)), dma((chips,)),
            dma((chips, n_blk)), dma((chips, n_blk)), dma((chips, n_blk)), dma((chips, n_blk)),
            dma((2, PIECES)), dma((2, PIECES)), dma((PIECES, chips)), dma((PIECES, chips)), dma((5,)),
        ],
        compiler_params=pltpu.CompilerParams(
            collective_id=0, has_side_effects=True, vmem_limit_bytes=60 * 1024 * 1024
        ),
        cost_estimate=pl.CostEstimate(
            flops=4 * lhs * rhs * groups * wide, bytes_accessed=4 * 1024 * 1024, transcendentals=0
        ),
        name="fused",
    )(block_owner, class_gain, precision, flat_images, store)
    return out.reshape(1, owned, per_block, cycles, angles)


def solution(mesh):
    return jax.shard_map(
        shards,
        mesh=mesh,
        in_specs=(P("dom", "blk", None), P("dom", None, None, "blk", None), P(), P(), P("dom")),
        out_specs=P("dom", None, None, "blk", None),
        check_vma=False,
    )
```

```python
import functools
import jax
import jax.numpy as jnp
from jax import lax
from jax.experimental import pallas as pl
from jax.experimental.pallas import tpu as pltpu
from jax.sharding import PartitionSpec as P

S = 64
S1 = 8
S2 = 8
G = 4
PIECES = 4
LANES = 128
NT = (((1,), (1,)), ((), ()))
MESH = pl.DeviceIdType.MESH


def roll_cycles(x, shift, angles):
    shift = shift % angles
    if shift == 0:
        return x
    parts = [
        pltpu.roll(x[:, c * angles : (c + 1) * angles], shift, 1)
        for c in range(x.shape[1] // angles)
    ]
    return jnp.concatenate(parts, axis=1)


def swap_halves(x, angles):
    half = angles // 2
    parts = []
    for c in range(x.shape[1] // angles):
        parts.append(x[:, c * angles + half : (c + 1) * angles])
        parts.append(x[:, c * angles : c * angles + half])
    return jnp.concatenate(parts, axis=1)


def every(ref, start, count, stride):
    return jnp.concatenate(
        [ref[h, pl.ds(start, count, stride=stride), :] for h in range(ref.shape[0])], axis=1
    )


def spread_lanes(op, x, width):
    shift = width
    while shift < x.shape[1]:
        x = op(x, pltpu.roll(x, shift, 1))
        shift *= 2
    return x


def kernel(
    n_dom, n_blk, angles, per_block, owned,
    owner_hbm, gain_hbm, prec_hbm, img_hbm, store_hbm, out_ref,
    owner_ref, gain_ref, prec_ref, img_ref, store_ref, imgf, blockf, minef, refs, rolled, turned, flat, norm, scores, got, weights, whole, parts, sib, zout, zin,
    ref_send, ref_recv, fwd_send, score_send, score_recv, w_send, w_recv,
    sib_send, sib_recv, z_send, z_recv, local,
):
    step = angles // S
    own = owned * per_block
    chips = n_dom // 2
    unit = 2 * own
    span = S2 * unit
    groups = rolled.shape[0]
    cycles = groups * G
    particles = img_ref.shape[0] // cycles
    wide = G * angles
    halves = angles // LANES
    pp = particles // n_blk
    blocks = store_ref.shape[0]
    me = lax.axis_index("dom")
    blk = lax.axis_index("blk")
    chip = me // 2
    core = me % 2
    sibling = chip * 2 + 1 - core
    far = [lax.rem(chip + o, chips) for o in range(1, chips)]
    pair = blk // 2
    blk_peers = [(1 - pair) * 2, (1 - pair) * 2 + 1, pair * 2 + 1 - blk % 2]

    store_in = pltpu.make_async_copy(store_hbm, store_ref, local.at[0])
    img_in = pltpu.make_async_copy(img_hbm, img_ref, local.at[1])
    small_in = [
        pltpu.make_async_copy(owner_hbm, owner_ref, local.at[2]),
        pltpu.make_async_copy(gain_hbm, gain_ref, local.at[3]),
        pltpu.make_async_copy(prec_hbm, prec_ref, local.at[4]),
    ]
    for copy in small_in:
        copy.start()
    store_in.start()
    img_in.start()
    barrier = pltpu.get_barrier_semaphore()
    for c in far:
        pl.semaphore_signal(barrier, inc=1, device_id={"dom": c * 2 + core}, device_id_type=MESH)
    pl.semaphore_signal(barrier, inc=1, device_id={"dom": sibling}, device_id_type=MESH)
    for b in blk_peers:
        pl.semaphore_signal(barrier, inc=1, device_id={"blk": b}, device_id_type=MESH)

    for copy in small_in:
        copy.wait()
    picks = [jnp.int32(0)] * owned
    seen = jnp.int32(0)
    for b in range(blocks):
        hit = (owner_ref[b] == me).astype(jnp.int32)
        for j in range(owned):
            take = jnp.logical_and(hit == 1, seen == j)
            picks[j] = jnp.where(take, jnp.int32(b), picks[j])
        seen = seen + hit
    store_in.wait()
    for j in range(owned):
        block = store_ref[picks[j]].astype(jnp.float32)
        for i in range(per_block):
            k = j * per_block + i
            gain = gain_ref[picks[j] * per_block + i]
            for h in range(halves):
                blockf[h, k * cycles : (k + 1) * cycles, :] = (
                    block[i * cycles : (i + 1) * cycles, h * LANES : (h + 1) * LANES] * gain
                )
    for r in range(cycles):
        g, rr = r // G, r % G
        minef[g // 2, (g % 2) * own : (g % 2 + 1) * own, rr * angles : (rr + 1) * angles] = (
            every(blockf, r, own, cycles)
        )
    refs[me] = minef[...].astype(jnp.bfloat16)

    pl.semaphore_wait(barrier, len(far) + 1 + len(blk_peers))

    def ref_copy(slot, target, send):
        return pltpu.make_async_remote_copy(
            src_ref=refs.at[slot], dst_ref=refs.at[slot], send_sem=send,
            recv_sem=ref_recv.at[slot], device_id={"dom": target}, device_id_type=MESH,
        )

    out_copies = [ref_copy(me, c * 2 + core, ref_send.at[o]) for o, c in enumerate(far)]
    out_copies.append(ref_copy(me, sibling, ref_send.at[chips - 1]))
    for copy in out_copies:
        copy.start()

    img_in.wait()

    def widen(i, carry):
        at = pl.ds(pl.multiple_of(i * 256, 256), 256)
        for h in range(halves):
            imgf[h, at, :] = img_ref[at, h * LANES : (h + 1) * LANES].astype(jnp.float32)
        return carry

    lax.fori_loop(0, particles * cycles // 256, widen, 0)

    def roll_images(g, carry):
        for rr in range(G):
            x = every(imgf, g * G + rr, particles, cycles).astype(jnp.bfloat16)
            for s1 in range(S1):
                r = roll_cycles(x, step * s1, angles)
                for j in range(n_blk):
                    at = j * pp * S1 + s1 * pp
                    rolled[g, at : at + pp, rr * angles : (rr + 1) * angles] = r[
                        j * pp : (j + 1) * pp, :
                    ]
        return carry

    lax.fori_loop(0, groups, roll_images, 0)
    lanes = pp * S1

    def score_copy(u, src, slot, target, o):
        return pltpu.make_async_remote_copy(
            src_ref=scores.at[u, src], dst_ref=got.at[u, slot], send_sem=score_send.at[u, o],
            recv_sem=score_recv.at[u, slot], device_id={"blk": target}, device_id_type=MESH,
        )

    fwd, score_copies = [], []
    for i in range(chips):
        u = lax.rem(chip + chips - i, chips)
        if i == 0:
            ref_copy(sibling, sibling, ref_send.at[chips - 1]).wait_recv()
        else:
            ref_copy(u * 2 + 1 - core, sibling, fwd_send.at[i - 1]).wait_recv()
        norm[...] = jnp.zeros_like(norm)
        scores[u] = jnp.zeros(scores.shape[1:], jnp.float32)

        def body(gp, carry, u=u):
            for e in range(2):
                y = refs[u * 2 + e, gp].astype(jnp.float32)
                for h in range(2):
                    flat[h, e * own : (e + 1) * own, :] = y[h * own : (h + 1) * own, :]
            for h in range(2):
                y = flat[h]
                half = 0.5 * jnp.sum(y * y, axis=1, keepdims=True)
                norm[...] += jnp.broadcast_to(half, norm.shape)
                y16 = y.astype(jnp.bfloat16)
                for s2 in range(S2 // 2):
                    t = roll_cycles(y16, -step * S1 * s2, angles)
                    turned[h, s2 * unit : (s2 + 1) * unit, :] = t
                    at = (s2 + S2 // 2) * unit
                    turned[h, at : at + unit, :] = swap_halves(t, angles)
            prod = lax.dot_general(
                turned[0], rolled[gp * 2], NT, preferred_element_type=jnp.float32
            ) + lax.dot_general(
                turned[1], rolled[gp * 2 + 1], NT, preferred_element_type=jnp.float32
            )
            for j in range(n_blk):
                scores[u, j] += prod[:, j * lanes : (j + 1) * lanes]
            return carry

        lax.fori_loop(0, groups // 4, body, 0)
        if i < chips - 1:
            slot = lax.rem(chip + chips - i - 1, chips) * 2 + core
            ref_copy(slot, slot, ref_send.at[i]).wait_recv()
            copy = ref_copy(slot, sibling, fwd_send.at[i])
            copy.start()
            fwd.append(copy)
        lax.fori_loop(groups // 4, groups // 2, body, 0)
        for j in range(n_blk):
            for s2 in range(S2):
                scores[u, j, s2 * unit : (s2 + 1) * unit, :] -= norm[...]
        copies = [score_copy(u, b, blk, b, o) for o, b in enumerate(blk_peers)]
        for o in (1, 0, 2):
            copies[o].start()
        score_copies += copies

    for u in range(chips):
        for o, b in enumerate(blk_peers):
            score_copy(u, b, b, b, o).wait_recv()
    total = jnp.concatenate(
        [
            functools.reduce(jnp.add, [got[u, b] for b in blk_peers], scores[u, blk])
            for u in range(chips)
        ],
        axis=0,
    )
    lane = lax.broadcasted_iota(jnp.int32, (8, lanes), 1) & (pp - 1)
    prec = jnp.zeros((8, lanes), jnp.float32)
    for i in range(pp):
        prec = jnp.where(lane == i, prec_ref[blk * pp + i], prec)
    logits = total * prec[0:1, :]
    top = jnp.broadcast_to(jnp.max(logits, axis=0, keepdims=True), (8, lanes))
    top = spread_lanes(jnp.maximum, top, pp)[0:1, :]
    e = jnp.exp(logits - top)
    mass = jnp.broadcast_to(jnp.sum(e, axis=0, keepdims=True), (8, lanes))
    mass = spread_lanes(jnp.add, mass, pp)[0:1, :]
    w = (e * (1.0 / mass)).astype(jnp.bfloat16)
    for u in range(chips):
        weights[u, blk] = w[u * span : (u + 1) * span, :]

    def w_copy(u, slot, target, o):
        return pltpu.make_async_remote_copy(
            src_ref=weights.at[u, slot], dst_ref=weights.at[u, slot], send_sem=w_send.at[u, o],
            recv_sem=w_recv.at[u, slot], device_id={"blk": target}, device_id_type=MESH,
        )

    order = far + [chip]
    w_copies = []
    for u in order:
        copies = [w_copy(u, blk, b, o) for o, b in enumerate(blk_peers)]
        for o in (1, 0, 2):
            copies[o].start()
        w_copies += copies

    per_piece = groups // PIECES
    part = chips // 2

    def sib_copy(h, q, which):
        return pltpu.make_async_remote_copy(
            src_ref=parts.at[which, h, q], dst_ref=sib.at[h, q], send_sem=sib_send.at[h, q],
            recv_sem=sib_recv.at[h, q], device_id={"dom": sibling}, device_id_type=MESH,
        )

    def z_copy(q, src, slot, target):
        return pltpu.make_async_remote_copy(
            src_ref=zout.at[q, src], dst_ref=zin.at[q, slot], send_sem=z_send.at[q, src],
            recv_sem=z_recv.at[q, slot], device_id={"dom": target * 2 + core}, device_id_type=MESH,
        )

    sib_copies, z_copies = [], []

    def finish(h, q):
        sib_copy(h, q, 1 - core).wait_recv()
        for i in range(part):
            at = h * part + i
            both = parts[core, h, q, i] + sib[h, q, i]
            if at == chips - 1:
                parts[core, h, q, i] = both
                continue
            zout[q, at] = both.reshape(per_piece * own, wide).astype(jnp.bfloat16)
            copy = z_copy(q, at, chip, order[at])
            copy.start()
            z_copies.append(copy)

    last = None
    for h in range(2):
        for i in range(part):
            u = order[h * part + i]
            for o, b in enumerate(blk_peers):
                w_copy(u, b, b, o).wait_recv()
            for j in range(n_blk):
                whole[i * span : (i + 1) * span, j * lanes : (j + 1) * lanes] = weights[u, j]
        for q in range(PIECES):

            def body(gi, carry, h=h, q=q):
                spread = jnp.dot(
                    whole[...], rolled[q * per_piece + gi], preferred_element_type=jnp.float32
                )
                for i in range(part):
                    base = i * span
                    fold = [
                        spread[base + s2 * unit : base + (s2 + 1) * unit, :]
                        + swap_halves(
                            spread[base + span // 2 + s2 * unit :][:unit, :], angles
                        )
                        for s2 in range(S2 // 2)
                    ]
                    running = fold[-1]
                    for s2 in reversed(range(S2 // 2 - 1)):
                        running = roll_cycles(running, step * S1, angles) + fold[s2]
                    for k in range(2):
                        parts[k, h, q, i, gi] = running[k * own : (k + 1) * own, :]
                return carry

            lax.fori_loop(0, per_piece, body, 0, unroll=True)
            copy = sib_copy(h, q, 1 - core)
            copy.start()
            sib_copies.append(copy)
            if last is not None:
                finish(*last)
            last = (h, q)
    finish(*last)

    for q in range(PIECES):
        total = parts[core, 1, q, part - 1].reshape(per_piece * own, wide)
        for c in far:
            z_copy(q, 0, c, c).wait_recv()
            total = total + zin[q, c].astype(jnp.float32)
        for gi in range(per_piece):
            for rr in range(G):
                out_ref[:, (q * per_piece + gi) * G + rr, :] = total[
                    gi * own : (gi + 1) * own, rr * angles : (rr + 1) * angles
                ]

    for copy in out_copies + fwd + score_copies + w_copies + sib_copies + z_copies:
        copy.wait_send()


def shards(images, ref_store, block_owner, class_gain, precision):
    particles, cycles, angles = images.shape
    n_dom = lax.axis_size("dom")
    n_blk = lax.axis_size("blk")
    blocks = block_owner.shape[0]
    per_block = ref_store.shape[2]
    owned = blocks // n_dom
    own = owned * per_block
    classes = blocks * per_block
    groups = cycles // G
    wide = G * angles
    chips = n_dom // 2
    unit = 2 * own
    pp = particles // n_blk
    lhs = S2 * classes
    rhs = S1 * particles
    per_piece = groups // PIECES

    flat_images = images.reshape(particles * cycles, angles)
    store = ref_store.reshape(blocks, per_block * cycles, angles)

    vmem = pl.BlockSpec(memory_space=pltpu.VMEM)
    hbm = pl.BlockSpec(memory_space=pl.ANY)
    bf16, f32 = jnp.bfloat16, jnp.float32
    dma = pltpu.SemaphoreType.DMA
    out = pl.pallas_call(
        functools.partial(kernel, n_dom, n_blk, angles, per_block, owned),
        in_specs=[hbm] * 5,
        out_specs=vmem,
        out_shape=jax.ShapeDtypeStruct((own, cycles, angles), f32),
        scratch_shapes=[
            pltpu.SMEM((blocks,), jnp.int32),
            pltpu.SMEM((classes,), f32),
            pltpu.SMEM((particles,), f32),
            pltpu.VMEM((particles * cycles, angles), bf16),
            pltpu.VMEM((blocks, per_block * cycles, angles), bf16),
            pltpu.VMEM((angles // LANES, particles * cycles, LANES), f32),
            pltpu.VMEM((angles // LANES, own * cycles, LANES), f32),
            pltpu.VMEM((groups // 2, 2 * own, wide), f32),
            pltpu.VMEM((n_dom, groups // 2, 2 * own, wide), bf16),
            pltpu.VMEM((groups, rhs, wide), bf16),
            pltpu.VMEM((2, S2 * unit, wide), bf16),
            pltpu.VMEM((2, unit, wide), f32),
            pltpu.VMEM((unit, pp * S1), f32),
            pltpu.VMEM((chips, n_blk, S2 * unit, pp * S1), f32),
            pltpu.VMEM((chips, n_blk, S2 * unit, pp * S1), f32),
            pltpu.VMEM((chips, n_blk, S2 * unit, pp * S1), bf16),
            pltpu.VMEM((lhs // 2, rhs), bf16),
            pltpu.VMEM((2, 2, PIECES, chips // 2, per_piece, own, wide), f32),
            pltpu.VMEM((2, PIECES, chips // 2, per_piece, own, wide), f32),
            pltpu.VMEM((PIECES, chips, per_piece * own, wide), bf16),
            pltpu.VMEM((PIECES, chips, per_piece * own, wide), bf16),
            dma((chips,)), dma((n_dom,)), dma((chips,)),
            dma((chips, n_blk)), dma((chips, n_blk)), dma((chips, n_blk)), dma((chips, n_blk)),
            dma((2, PIECES)), dma((2, PIECES)), dma((PIECES, chips)), dma((PIECES, chips)), dma((5,)),
        ],
        compiler_params=pltpu.CompilerParams(
            collective_id=0, has_side_effects=True, vmem_limit_bytes=60 * 1024 * 1024
        ),
        cost_estimate=pl.CostEstimate(
            flops=4 * lhs * rhs * groups * wide, bytes_accessed=4 * 1024 * 1024, transcendentals=0
        ),
        name="fused",
    )(block_owner, class_gain, precision, flat_images, store)
    return out.reshape(1, owned, per_block, cycles, angles)


def solution(mesh):
    return jax.shard_map(
        shards,
        mesh=mesh,
        in_specs=(P("dom", "blk", None), P("dom", None, None, "blk", None), P(), P(), P("dom")),
        out_specs=P("dom", None, None, "blk", None),
        check_vma=False,
    )
```
